256 devices in a mesh: dp: 4 (over y), expert: 64 (over z, x, core).
Axes of the slice: x: 4, y: 4, z: 8, core: 2. Of those that a mesh axis runs over, the one named last changes fastest.
Arguments:
- out_grad: bfloat16 [40960, 3584], P('expert', 'dp'), may hold values from -0.3125 to 0.3125
- routes: int32 [40960, 4], P('expert'), may hold values from 0 to 127, all different within a row; in each aligned block of 640 rows (0 to 639, 640 to 1279, ...) at most 30 rows name the same one
- gates: float32 [40960, 4], P('expert'), may hold values from 0.05 to 1
- dup_owner: int32 [64], replicated, may hold values from 0 to 63
- hidden: bfloat16 [64, 64, 2, 30, 1024], P('expert', None, None, None, 'dp'), may hold values from -6 to 6
- moment1: bfloat16 [64, 1024, 3584], P(None, 'expert', 'dp'), may hold values from -0.625 to 0.625
- moment2: bfloat16 [64, 1024, 3584], P(None, 'expert', 'dp'), may hold values from 0.0099487305 to 0.29882812
- value_grad: bfloat16 [40960, 4096], P('expert', 'dp'), may hold values from -2 to 2
- value_proj: bfloat16 [512, 4096], P(None, 'dp'), may hold values from -0.25 to 0.25
Outputs:
- slot_steps: bfloat16 [64, 2, 1024, 3584], P('expert', None, None, 'dp')
- latent_grad: bfloat16 [512, 40960], P('dp', 'expert')
The draws below stay inside these ranges and needn't reach their ends.
Inputs may be any that keep to these rules, and one draw needn't show every extreme that they name: Among the routes of one token group's rows, a token names distinct slots, a slot is named at most 30 times, a bound that some block reaches.
All inputs are finite; a program needn't handle non-finite values.
Results may differ from the reference program's by a relative error of at most 0.0065.
Values may be sent and summed in bfloat16 or wider, within the bound.
A program may use at most 128 MiB of HBM per device.

```python
import math
import jax
import jax.numpy as jnp
import numpy as np
from jax import lax

D = 3584
FW = 1024
HEADS = 32
HV = 128
LAT = 512
TOPK = 4
TOK_DEV = 640
TOKENS = 40960
EXPERTS = 64
SLOTS = 128
CAP = 30
N_EXPERT = 64


def set_ends(result, key, low, top_value):
    longest = result.shape.index(max(result.shape))
    spots = []
    for shift in (0, 1):
        where = [jax.random.randint(jax.random.fold_in(key, axis), (), 0, length) for axis, length in enumerate(result.shape)]
        where[longest] = (where[longest] + shift) % result.shape[longest]
        spots.append(tuple(where))
    return result.at[spots[0]].set(low).at[spots[1]].set(top_value)


def block_scale(rng, extent, split, least, largest):
    level, own = 1.0, jax.random.fold_in(rng, 6)
    for axis_at, parts in split:
        draws = jnp.exp(jax.random.uniform(jax.random.fold_in(own, axis_at), (parts,), jnp.float32, least / len(split), largest / len(split)))
        level = level * jnp.repeat(draws, extent[axis_at] // parts).reshape([-1 if axis == axis_at else 1 for axis in range(len(extent))])
    return level


def rank_bounds(number_of, lean):
    portions = [(1 << 20) // math.isqrt(standing ** lean) + 1 for standing in range(1, number_of + 1)]
    scale = 1 + sum(portions) // (1 << 30)
    return np.cumsum(np.array([max(1, weight // scale) for weight in portions]))


def ranked_ids(own_key, shape, count, lean):
    listing = rank_bounds(count, lean)
    ticket = jax.random.randint(jax.random.fold_in(own_key, 1), shape, 0, int(listing[count - 1]))
    rank = jnp.searchsorted(jnp.asarray(listing, jnp.int32), ticket, side="right")
    return jax.random.permutation(jax.random.fold_in(own_key, 2), count)[rank].astype(jnp.int32)


def assign_block(stream_key, own, number, rows, count, top, bound, lean):
    ranking = jax.random.permutation(stream_key, count)
    heavy_load, usual = load_shares(count, rows * top, bound, lean, True), load_shares(count, rows * top, bound, lean, False)
    places = jnp.arange(count)

    def named(tallies, rotation):
        used = int((tallies > 0).sum())
        fixed = max(1, used // 4)
        shifted = fixed + (places - fixed + rotation * (used - fixed)) % max(1, count - fixed)
        return jnp.zeros((count,), jnp.int32).at[ranking[jnp.where(places < fixed, places, shifted)]].set(jnp.asarray(tallies, jnp.int32))

    tallies = jnp.where(number % 4 == 0, named(heavy_load, number // 4), named(usual, number - number // 4 - 1))
    mixed = jax.random.permutation(jax.random.fold_in(own, 3), count)
    donor, receiver = mixed[0:count // 2 * 2:2], mixed[1:count // 2 * 2:2]
    slack = jnp.minimum(tallies[donor] - 1, bound - tallies[receiver]) // 2
    slack = jnp.where((donor == ranking[0]) | (receiver == ranking[0]) | (tallies[receiver] == 0), 0, jnp.maximum(slack, 0))
    shifted = jax.random.randint(jax.random.fold_in(own, 4), (count // 2,), 0, 1 << 20) % (slack + 1)
    tallies = tallies.at[donor].add(-shifted).at[receiver].add(shifted)
    items = jnp.searchsorted(jnp.cumsum(tallies), jnp.arange(rows * top), side="right").astype(jnp.int32)
    listing = items.reshape(top, rows).T
    listing = listing[jax.random.permutation(jax.random.fold_in(own, 1), rows)]
    rotation = jax.random.randint(jax.random.fold_in(own, 2), (rows, 1), 0, top)
    return jnp.take_along_axis(listing, (jnp.arange(top)[None, :] + rotation) % top, axis=1)


def load_shares(number_of, total, bound, lean, full):
    portions = [(1 << 20) // math.isqrt(rank ** lean) + 1 for rank in range(1, number_of + 1)]
    largest = bound if full else min(bound, max(-(-total // number_of), total * portions[0] // sum(portions)))
    least = 1 if total - largest >= number_of - 1 else 0
    counts, rest = [largest] + [least] * (number_of - 1), total - largest - least * (number_of - 1)
    while rest > 0:
        free = [i for i in range(1, number_of) if counts[i] < largest] or [i for i in range(1, number_of) if counts[i] < bound]
        mass, budget = sum([portions[i] for i in free]), rest
        for i in free:
            more = min(bound - counts[i], max(1, budget * portions[i] // mass), rest)
            counts[i] = counts[i] + more
            rest = rest - more
    return np.array(counts)


def bell_draw(key, shape, spread, reach, shards=(), kind=jnp.bfloat16):
    entries = jax.random.normal(key, shape, jnp.float32) * spread
    if len(shards) > 0:
        entries = block_scale(key, shape, shards, -0.22, 0.18) * entries
    return jnp.clip(entries, min=-reach, max=reach).astype(kind)


def setup_inputs(seed: int = 0) -> dict:
    key_of = jax.random.split(jax.random.key(seed), 10)
    out_grad = bell_draw(key_of[0], (TOKENS, D), (2.0 / (TOPK * TOK_DEV / 2) ** 0.5), 0.3125, ((0, 64), (1, 4)))
    routes_keys = jax.random.split(jax.random.fold_in(key_of[1], 1), TOKENS // TOK_DEV)
    routes_turns = jax.random.permutation(jax.random.fold_in(key_of[1], 3), TOKENS // TOK_DEV)
    routes = jax.vmap(lambda own, number: assign_block(jax.random.fold_in(key_of[1], 2), own, number, TOK_DEV, SLOTS, TOPK, CAP, 2))(routes_keys, routes_turns).reshape((TOKENS, TOPK))
    gates = jnp.clip(0.05 + 0.95 * jax.random.uniform(key_of[2], (TOKENS, TOPK), jnp.float32) ** block_scale(key_of[2], (TOKENS, TOPK), ((0, 64),), -0.2, 0.2), 0.05, 1.0)
    dup_owner = set_ends(ranked_ids(key_of[3], (N_EXPERT,), EXPERTS, 2), jax.random.fold_in(key_of[3], 3), 0, EXPERTS - 1).astype(jnp.int32)
    hidden = bell_draw(key_of[4], (N_EXPERT, N_EXPERT, 2, CAP, FW), 1.0, 6.0, ((0, 64), (4, 4)))
    moment1 = bell_draw(key_of[5], (EXPERTS, FW, D), 0.1, 0.625, ((1, 64), (2, 4)))
    moment2 = jnp.clip(jnp.exp(math.log(0.29882812) - 3.4024236 * jax.random.uniform(key_of[6], (EXPERTS, FW, D), jnp.float32) ** block_scale(key_of[6], (EXPERTS, FW, D), ((1, 64), (2, 4)), -0.2, 0.2)), 0.0099487305, 0.29882812).astype(jnp.bfloat16)
    value_grad = bell_draw(key_of[7], (TOKENS, HEADS * HV), 0.35, 2.0, ((0, 64), (1, 4)))
    value_proj = bell_draw(key_of[8], (LAT, HEADS * HV), LAT ** -0.5, 0.25, ((1, 4),))
    return {"out_grad": out_grad, "routes": routes, "gates": gates, "dup_owner": dup_owner, "hidden": hidden, "moment1": moment1, "moment2": moment2, "value_grad": value_grad, "value_proj": value_proj}


beta_first = 0.9
beta_second = 0.95
adam_eps = 1e-08
bias_first = 1.0 - 0.9 ** 50 * 0.9 ** 50
bias_second = 1.0 - 0.95 ** 50 * 0.95 ** 50

def route_places(group_routes):
    flat_routes = group_routes.reshape(-1)
    onehot = (flat_routes[:, None] == jnp.arange(SLOTS, dtype=jnp.int32)[None, :]).astype(jnp.int32)
    earlier = (jnp.cumsum(onehot, axis=0) - onehot).astype(jnp.int32)
    route_rank = lax.optimization_barrier(jnp.sum(earlier * onehot, axis=1)).astype(jnp.int32)
    return flat_routes * CAP + route_rank

def place_values(base, target, values):
    return base.at[target].set(values)

def take_rows(table, chosen):
    return table[chosen]

def adam_step(moments):
    first_moment, second_moment, gradient = moments
    first_moment = beta_first * first_moment.astype(jnp.float32) + (1.0 - beta_first) * gradient
    second_moment = beta_second * second_moment.astype(jnp.float32) + (1.0 - beta_second) * gradient * gradient
    step_value = first_moment / bias_first / (jnp.sqrt(second_moment / bias_second) + adam_eps)
    return step_value.astype(jnp.bfloat16)

def reference(out_grad, routes, gates, dup_owner, hidden, moment1, moment2, value_grad, value_proj):
    targets = jax.vmap(route_places)(routes.reshape(N_EXPERT, TOK_DEV, TOPK))
    token_ids = jnp.broadcast_to(jnp.repeat(jnp.arange(TOK_DEV, dtype=jnp.int32), TOPK)[None, :], targets.shape)
    empty_ids = jnp.full((N_EXPERT, SLOTS * CAP), -1, jnp.int32)
    source_token = jax.vmap(place_values)(empty_ids, targets, token_ids)
    empty_gates = jnp.zeros((N_EXPERT, SLOTS * CAP), jnp.float32)
    source_gate = jax.vmap(place_values)(empty_gates, targets, gates.reshape(N_EXPERT, TOK_DEV * TOPK))
    source_token = source_token.reshape(N_EXPERT, N_EXPERT, 2 * CAP)
    source_gate = source_gate.reshape(N_EXPERT, N_EXPERT, 2 * CAP)
    tokens_by_group = out_grad.reshape(N_EXPERT, TOK_DEV, D)

    def absorb(total, group_index):
        chosen = source_token[:, group_index]
        weight = source_gate[:, group_index]
        rows = jax.vmap(take_rows)(tokens_by_group, jnp.maximum(chosen, 0))
        scaled = jnp.where((chosen >= 0)[:, :, None], weight[:, :, None] * rows.astype(jnp.float32), 0.0)
        scaled = scaled.astype(jnp.bfloat16).reshape(N_EXPERT, 2, CAP, D)
        terms = jnp.einsum('swcf,swcd->wfd', hidden[group_index].astype(jnp.float32), scaled.astype(jnp.float32))
        total = total.at[group_index].add(terms[0])
        total = total.at[dup_owner[group_index]].add(terms[1])
        return (total, None)
    total, _ = lax.scan(absorb, jnp.zeros((EXPERTS, FW, D), jnp.float32), jnp.arange(N_EXPERT, dtype=jnp.int32))
    expert_step = lax.map(adam_step, (moment1, moment2, total))
    slot_steps = jnp.stack([expert_step, expert_step[dup_owner]], axis=1)
    latent_grad = jnp.dot(value_proj, value_grad.T, preferred_element_type=jnp.float32).astype(jnp.bfloat16)
    return (slot_steps, latent_grad)
```

```python
import functools

import jax
import jax.numpy as jnp
from jax import lax
from jax.experimental import pallas as pl
from jax.experimental.pallas import tpu as pltpu
from jax.sharding import PartitionSpec as P

beta_first = 0.9
beta_second = 0.95
adam_eps = 1e-08
bias_first = 1.0 - 0.9**50 * 0.9**50
bias_second = 1.0 - 0.95**50 * 0.95**50

PLANES = 8
PEERS = 8
ROWS = 16
POS = 32
TOKENS = 640
FPART = 256
WIDTH = 896
CHUNKS = ((0, 256), (256, 256), (512, 256), (768, 128))
N = len(CHUNKS)
HALF = TOKENS // 2
MESH = pl.DeviceIdType.MESH
F32 = jnp.float32
BF16 = jnp.bfloat16


def kernel(
    og,
    meta,
    hid,
    trow,
    m1,
    m2,
    out,
    *refs,
):
    relay_x, relay_s, refs = refs[:N], refs[N : 2 * N], refs[2 * N :]
    tok, refs = refs[:N], refs[N:]
    rows_in, refs = refs[:N], refs[N:]
    grad_in, refs = refs[:N], refs[N:]
    (
        metas,
        onehot,
        gate_col,
        rows_out,
        hid_t,
        part_out,
        step_out,
        mom,
        kron,
        kron_t,
        sem_meta,
        sem_ring,
        sem_hid,
        sem_rows,
        sem_px,
        sem_pz,
        sem_sz,
        sem_sx,
        sem_local,
        sem_own,
    ) = refs
    me = lax.axis_index("expert")
    y = lax.axis_index("dp")
    z = me // PEERS
    p = me % PEERS

    def plane(d):
        return lax.rem(z + d + PLANES, PLANES)

    def peer(d):
        return lax.rem(p + d + PEERS, PEERS)

    def dev_z(to):
        return {"expert": to * PEERS + p}

    def dev_p(to):
        return {"expert": z * PEERS + to}

    def dev_y(d):
        return {"dp": lax.rem(y + d + 4, 4)}

    def remote(src, dst, sems, index_out, index_in, device):
        return pltpu.make_async_remote_copy(
            src_ref=src,
            dst_ref=dst,
            send_sem=sems.at[(0,) + index_out],
            recv_sem=sems.at[(1,) + index_in],
            device_id=device,
            device_id_type=MESH,
        )

    def others(body):
        def step(i, carry):
            body(i)
            return carry

        lax.fori_loop(1, 8, step, 0)

    barrier = pltpu.get_barrier_semaphore()

    def greet(i):
        pl.semaphore_signal(barrier, inc=1, device_id=dev_z(plane(i)), device_id_type=MESH)
        pl.semaphore_signal(barrier, inc=1, device_id=dev_p(peer(i)), device_id_type=MESH)

    others(greet)
    for d in (1, -1):
        pl.semaphore_signal(barrier, inc=1, device_id=dev_y(d), device_id_type=MESH)

    def local(src, dst, index):
        return pltpu.make_async_copy(src, dst, sem_local.at[index])

    own_tok = [
        local(og.at[:, pl.ds(CHUNKS[k][0], CHUNKS[k][1])], tok[k].at[z], k) for k in range(N)
    ]
    load_hid = local(hid, rows_out.at[1], N)
    load_meta = local(meta, metas.at[z], N + 1)

    def load_moments(k):
        c0, dc = CHUNKS[k]
        return [
            local(
                m.at[:, pl.ds(c0, dc)],
                mom.at[k % 2, i, :, pl.ds(0, dc)],
                N + 2 + 2 * (k % 2) + i,
            )
            for i, m in enumerate((m1, m2))
        ]

    load_hid.start()
    load_meta.start()
    for copy in own_tok:
        copy.start()
    for k in (0, 1):
        for copy in load_moments(k):
            copy.start()

    pl.semaphore_wait(barrier, 16)

    def meta_copy(i):
        return remote(meta, metas.at[z], sem_meta, (i,), (i,), dev_z(plane(i)))

    others(lambda i: meta_copy(i).start())

    def ring_send(k, way, step, half):
        c0, dc = CHUNKS[k]
        sign = 1 - 2 * way
        block = plane(-sign * (step - 1))
        rows = pl.ds(half * HALF, HALF)
        source = og.at[rows, pl.ds(c0, dc)] if step == 1 else tok[k].at[block, rows]
        index = (k, way, step - 1, half)
        return remote(
            source, tok[k].at[block, rows], sem_ring, index, index, dev_z(plane(sign))
        )

    def ring_arrival(k, way, step, half):
        sign = 1 - 2 * way
        block = plane(-sign * step)
        rows = pl.ds(half * HALF, HALF)
        index = (k, way, step - 1, half)
        view = tok[k].at[block, rows]
        return remote(view, view, sem_ring, index, index, dev_z(plane(sign)))

    def ring_parts(step):
        return [(way, half) for half in (0, 1) for way in (0, 1) if step < 4 or half == way]

    def ring_begin(k):
        for way, half in ring_parts(1):
            ring_send(k, way, 1, half).start()

    ring_begin(0)

    load_hid.wait()

    def transpose_piece(i, carry):
        w = i // PEERS
        q = lax.rem(i, PEERS)
        piece = rows_out[1, q, w].reshape(PLANES * POS, FPART)
        hid_t[w, y, q] = piece.T
        return carry

    lax.fori_loop(0, 2 * PEERS, transpose_piece, 0)

    def hid_copy(index, w, part, d):
        view = hid_t.at[w, part]
        return remote(view, view, sem_hid, (index,), (index,), dev_y(d))

    def y_part(d):
        return lax.rem(y + d + 4, 4)

    hid_first = [(0, 0, 1), (1, 1, 1), (2, 0, -1), (3, 1, -1)]
    for index, w, d in hid_first:
        hid_copy(index, w, y, d).start()

    load_meta.wait()
    others(lambda i: remote(meta, metas.at[plane(-i)], sem_meta, (i,), (i,), dev_z(z)).wait_recv())
    earlier = (
        lax.broadcasted_iota(jnp.int32, (TOKENS, TOKENS), 0)
        < lax.broadcasted_iota(jnp.int32, (TOKENS, TOKENS), 1)
    ).astype(F32).astype(BF16)

    def build_plane(i, carry):
        slot_of = (lax.broadcasted_iota(jnp.int32, (16, TOKENS), 0) + z * 16).astype(F32)
        named = jnp.zeros((16, TOKENS), F32)
        gate = jnp.zeros((16, TOKENS), F32)
        table = metas[i]
        for k in range(4):
            match = slot_of == table[k : k + 1, :]
            named = jnp.where(match, 1.0, named)
            gate = jnp.where(match, table[4 + k : 5 + k, :], gate)
        rank = jnp.dot(named.astype(BF16), earlier, preferred_element_type=F32)
        rank = jnp.where(named > 0.5, rank, -1.0)
        position = lax.broadcasted_iota(jnp.int32, (POS, TOKENS), 0).astype(F32)
        for s in range(16):
            chosen = position == rank[s : s + 1, :]
            onehot[i, s * POS : (s + 1) * POS, :] = jnp.where(chosen, 1.0, 0.0).astype(BF16)
            weight = jnp.sum(
                jnp.where(chosen, gate[s : s + 1, :], 0.0), axis=1, keepdims=True
            )
            gate_col[i, s * POS : (s + 1) * POS, :] = jnp.broadcast_to(weight, (POS, 128))
        return carry

    lax.fori_loop(0, PLANES, build_plane, 0)

    def gather(k, source):
        dc = CHUNKS[k][1]
        picked = jnp.dot(onehot[source], tok[k][source], preferred_element_type=F32)
        for part in range(dc // 128):
            lanes = slice(part * 128, (part + 1) * 128)
            scaled = (picked[:, lanes] * gate_col[source]).astype(BF16)
            scaled = scaled.reshape(PEERS, 2, POS, 128)
            rows_out[k % 2, :, :, source, :, lanes] = scaled

    def rows_copy(k, to, index):
        dc = CHUNKS[k][1]
        return remote(
            rows_out.at[k % 2, to, :, :, :, pl.ds(0, dc)],
            rows_in[k].at[:, p],
            sem_rows,
            (k, index),
            (k, index),
            dev_p(to),
        )

    def rows_arrival(k, source, index):
        view = rows_in[k].at[:, source]
        return remote(view, view, sem_rows, (k, index), (k, index), dev_p(source))

    def own(src, dst, stage, k):
        return pltpu.make_async_copy(src, dst, sem_own.at[stage, k])

    def rows_own(k):
        dc = CHUNKS[k][1]
        return own(rows_out.at[k % 2, p, :, :, :, pl.ds(0, dc)], rows_in[k].at[:, p], 0, k)

    def rows_sent(k):
        others(lambda i: rows_copy(k, peer(i), i).wait_send())

    def stage_ring(k):
        own_tok[k].wait()
        if k >= 2:
            rows_sent(k - 2)
        gather(k, z)
        for step in (1, 2, 3, 4):
            for way, half in ring_parts(step):
                ring_arrival(k, way, step, half).wait_recv()
                if step < 3 or (step == 3 and half == way):
                    ring_send(k, way, step + 1, half).start()
            if step == 1 and k + 1 < N:
                ring_begin(k + 1)
            gather(k, plane(step))
            if step < 4:
                gather(k, plane(-step))
        rows_own(k).start()
        others(lambda i: rows_copy(k, peer(i), i).start())

    def part_view(k, to):
        return part_out.at[k % 2, to, :, :, :, pl.ds(0, CHUNKS[k][1])]

    def part_copy(k, to, index):
        return remote(
            part_view(k, to), relay_x[k].at[:, p], sem_px, (k, index), (k, index), dev_p(to)
        )

    def part_arrival(k, source, index):
        view = relay_x[k].at[:, source]
        return remote(view, view, sem_px, (k, index), (k, index), dev_p(source))

    def part_own(k):
        return own(part_view(k, p), relay_x[k].at[:, p], 1, k)

    def stage_matmul(k):
        dc = CHUNKS[k][1]
        rows_own(k).wait()
        others(lambda i: rows_arrival(k, peer(-i), i).wait_recv())
        if k >= 2:
            others(lambda i: part_copy(k - 2, peer(i), i).wait_send())

        def block(i, carry):
            w = lax.rem(i, 2)
            part = lax.rem(y + i // 2, 4)
            total = jnp.zeros((FPART, dc), F32)
            for q in range(PEERS):
                total += jnp.dot(
                    hid_t[w, part, q],
                    rows_in[k][w, q].reshape(PLANES * POS, dc),
                    preferred_element_type=F32,
                )
            rounded = total.astype(BF16).reshape(2, PEERS, ROWS, dc)
            for h in range(2):
                for q in range(PEERS):
                    part_out[k % 2, q, w, 2 * part + h, :, 0:dc] = rounded[h, q]
            return carry

        lax.fori_loop(0, 8, block, 0)
        part_own(k).start()
        others(lambda i: part_copy(k, peer(i), i).start())

    def grad_copy(k, to, index):
        return remote(
            relay_x[k].at[:, :, to],
            grad_in[k].at[:, z],
            sem_pz,
            (k, index),
            (k, index),
            dev_z(to),
        )

    def grad_arrival(k, source, index):
        view = grad_in[k].at[:, source]
        return remote(view, view, sem_pz, (k, index), (k, index), dev_z(source))

    def grad_own(k):
        return own(relay_x[k].at[:, :, z], grad_in[k].at[:, z], 2, k)

    def stage_forward(k):
        part_own(k).wait()
        others(lambda i: part_arrival(k, peer(-i), i).wait_recv())
        others(lambda i: grad_copy(k, plane(i), i).start())
        grad_own(k).start()

    def step_view(k, to):
        return step_out.at[k % 2, :, to, :, :, pl.ds(0, CHUNKS[k][1])]

    def step_copy(k, to, index):
        return remote(
            step_view(k, to), relay_s[k].at[:, z], sem_sz, (k, index), (k, index), dev_z(to)
        )

    def step_arrival(k, source, index):
        view = relay_s[k].at[:, source]
        return remote(view, view, sem_sz, (k, index), (k, index), dev_z(source))

    def step_own(k):
        return own(step_view(k, z), relay_s[k].at[:, z], 3, k)

    tile = 256
    per_tile = tile // (PEERS * ROWS)

    def stage_adam(k):
        dc = CHUNKS[k][1]
        grad_own(k).wait()
        others(lambda i: grad_arrival(k, plane(-i), i).wait_recv())
        if k >= 2:
            others(lambda i: step_copy(k - 2, plane(i), i).wait_send())
        for copy in load_moments(k):
            copy.wait()

        def block(i, carry):
            rows = pl.ds(pl.multiple_of(i * tile, tile), tile)
            planes = pl.ds(i * per_tile, per_tile)
            twins = grad_in[k][1].reshape(PLANES * PEERS * ROWS, dc)
            gradient = grad_in[k][0, planes].reshape(tile, dc).astype(F32)
            gradient += jnp.dot(kron[rows, :], twins, preferred_element_type=F32)
            first = beta_first * mom[k % 2, 0, rows, 0:dc].astype(F32)
            first += (1.0 - beta_first) * gradient
            second = beta_second * mom[k % 2, 1, rows, 0:dc].astype(F32)
            second += (1.0 - beta_second) * gradient * gradient
            value = first / bias_first / (jnp.sqrt(second / bias_second) + adam_eps)
            value = value.astype(BF16).reshape(per_tile, PEERS, ROWS, dc)
            step_out[k % 2, 0, planes, :, :, 0:dc] = value
            return carry

        lax.fori_loop(0, PLANES // per_tile, block, 0)

        def twin(i, carry):
            rows = pl.ds(pl.multiple_of(i * tile, tile), tile)
            planes = pl.ds(i * per_tile, per_tile)
            steps = step_out[k % 2, 0, :, :, :, 0:dc].reshape(PLANES * PEERS * ROWS, dc)
            value = jnp.dot(kron_t[rows, :], steps, preferred_element_type=F32)
            value = value.astype(BF16).reshape(per_tile, PEERS, ROWS, dc)
            step_out[k % 2, 1, planes, :, :, 0:dc] = value
            return carry

        lax.fori_loop(0, PLANES // per_tile, twin, 0)
        step_own(k).start()
        others(lambda i: step_copy(k, plane(i), i).start())
        if k + 2 < N:
            for copy in load_moments(k + 2):
                copy.start()

    def out_view(k, source):
        return out.at[:, :, source, :, pl.ds(CHUNKS[k][0], CHUNKS[k][1])]

    def out_copy(k, to, index):
        return remote(
            relay_s[k].at[:, :, to], out_view(k, p), sem_sx, (k, index), (k, index), dev_p(to)
        )

    def out_arrival(k, source, index):
        view = out_view(k, source)
        return remote(view, view, sem_sx, (k, index), (k, index), dev_p(source))

    def out_own(k):
        return own(relay_s[k].at[:, :, p], out_view(k, p), 4, k)

    def stage_return(k):
        step_own(k).wait()
        others(lambda i: step_arrival(k, plane(-i), i).wait_recv())
        out_own(k).start()
        others(lambda i: out_copy(k, peer(i), i).start())

    def build_kron():
        target = trow[...]
        for i in range(PLANES):
            rows = lax.broadcasted_iota(jnp.int32, (128, 1024), 0) + i * 128
            kron[i * 128 : (i + 1) * 128, :] = (
                jnp.where(rows == target, 1.0, 0.0).astype(BF16)
            )
            column = jnp.broadcast_to(target[:, i * 128 : (i + 1) * 128].astype(F32), (128, 128)).T
            for j in range(PLANES):
                lanes = lax.broadcasted_iota(jnp.int32, (128, 128), 1) + j * 128
                kron_t[i * 128 : (i + 1) * 128, j * 128 : (j + 1) * 128] = jnp.where(
                    lanes.astype(F32) == column, 1.0, 0.0
                ).astype(BF16)

    hid_second = [(4, 0, y_part(-1), 1), (5, 1, y_part(1), -1)]

    def forward_hidden():
        hid_copy(0, 0, y_part(-1), 1).wait_recv()
        hid_copy(4, 0, y_part(-1), 1).start()
        hid_copy(3, 1, y_part(1), -1).wait_recv()
        hid_copy(5, 1, y_part(1), -1).start()

    def finish_hidden():
        hid_copy(1, 1, y_part(-1), 1).wait_recv()
        hid_copy(2, 0, y_part(1), -1).wait_recv()
        hid_copy(4, 0, y_part(2), 1).wait_recv()
        hid_copy(5, 1, y_part(2), -1).wait_recv()

    stage_ring(0)
    forward_hidden()
    build_kron()
    stage_ring(1)
    finish_hidden()
    stage_matmul(0)
    stage_ring(2)
    stage_forward(0)
    stage_matmul(1)
    stage_ring(3)
    stage_forward(1)
    stage_matmul(2)
    stage_adam(0)
    stage_forward(2)
    stage_matmul(3)
    stage_adam(1)
    stage_return(0)
    stage_forward(3)
    stage_adam(2)
    stage_return(1)
    stage_adam(3)
    stage_return(2)
    stage_return(3)

    others(lambda i: meta_copy(i).wait_send())
    for index, w, d in hid_first:
        hid_copy(index, w, y, d).wait_send()
    for index, w, part, d in hid_second:
        hid_copy(index, w, part, d).wait_send()
    for k in range(N):
        for step in (1, 2, 3, 4):
            for way, half in ring_parts(step):
                ring_send(k, way, step, half).wait_send()
        others(lambda i: grad_copy(k, plane(i), i).wait_send())
        others(lambda i: out_copy(k, peer(i), i).wait_send())
        if k >= N - 2:
            rows_sent(k)
            others(lambda i: part_copy(k, peer(i), i).wait_send())
            others(lambda i: step_copy(k, plane(i), i).wait_send())
        others(lambda i: out_arrival(k, peer(-i), i).wait_recv())
        out_own(k).wait()


def expert_steps(og, meta, hid, trow, m1, m2):
    anywhere = pl.BlockSpec(memory_space=pl.ANY)
    relays = [
        jax.ShapeDtypeStruct((2, PEERS, PLANES, ROWS, dc), BF16) for _, dc in CHUNKS
    ]
    returns = [
        jax.ShapeDtypeStruct((2, PLANES, PEERS, ROWS, dc), BF16) for _, dc in CHUNKS
    ]
    shape = jax.ShapeDtypeStruct((2, PLANES, PEERS, ROWS, WIDTH), BF16)
    widest = max(dc for _, dc in CHUNKS)
    dma = pltpu.SemaphoreType.DMA
    scratch = [pltpu.VMEM((PLANES, TOKENS, dc), BF16) for _, dc in CHUNKS]
    scratch += [pltpu.VMEM((2, PEERS, PLANES, POS, dc), BF16) for _, dc in CHUNKS]
    scratch += [pltpu.VMEM((2, PLANES, PEERS, ROWS, dc), BF16) for _, dc in CHUNKS]
    scratch += [
        pltpu.VMEM((PLANES, 8, TOKENS), F32),
        pltpu.VMEM((PLANES, 16 * POS, TOKENS), BF16),
        pltpu.VMEM((PLANES, 16 * POS, 128), F32),
        pltpu.VMEM((2, PEERS, 2, PLANES, POS, widest), BF16),
        pltpu.VMEM((2, 4, PEERS, FPART, PLANES * POS), BF16),
        pltpu.VMEM((2, PEERS, 2, PLANES, ROWS, widest), BF16),
        pltpu.VMEM((2, 2, PLANES, PEERS, ROWS, widest), BF16),
        pltpu.VMEM((2, 2, PLANES * PEERS * ROWS, widest), BF16),
        pltpu.VMEM((1024, 1024), BF16),
        pltpu.VMEM((1024, 1024), BF16),
        dma((2, 8)),
        dma((2, N, 2, 4, 2)),
        dma((2, 6)),
        dma((2, N, 8)),
        dma((2, N, 8)),
        dma((2, N, 8)),
        dma((2, N, 8)),
        dma((2, N, 8)),
        dma((N + 6,)),
        dma((5, N)),
    ]
    results = pl.pallas_call(
        kernel,
        out_shape=[shape] + relays + returns,
        in_specs=[anywhere, anywhere, anywhere, pl.BlockSpec(memory_space=pltpu.VMEM), anywhere, anywhere],
        out_specs=[anywhere] * (1 + 2 * N),
        scratch_shapes=scratch,
        compiler_params=pltpu.CompilerParams(
            collective_id=0, has_side_effects=True, vmem_limit_bytes=62 * 1024 * 1024
        ),
        cost_estimate=pl.CostEstimate(
            flops=50_000_000_000, bytes_accessed=60_000_000, transcendentals=2_000_000
        ),
    )(og, meta, hid, trow, m1, m2)
    return results[0]


def shards(out_grad, routes, gates, dup_owner, hidden, moment1, moment2, value_grad, value_proj):
    experts = PLANES * PEERS
    meta = jnp.concatenate([routes.astype(F32), gates], axis=1).T
    hid = hidden[0].reshape(PLANES, PEERS, 2, hidden.shape[3], FPART)
    hid = jnp.pad(
        hid.transpose(1, 2, 0, 3, 4), ((0, 0), (0, 0), (0, 0), (0, POS - hidden.shape[3]), (0, 0))
    )
    trow = (dup_owner[:, None] * ROWS + jnp.arange(ROWS, dtype=jnp.int32)[None, :]).reshape(1, -1)
    steps = expert_steps(
        out_grad,
        meta,
        hid,
        trow,
        moment1.reshape(experts * ROWS, WIDTH),
        moment2.reshape(experts * ROWS, WIDTH),
    )
    latent_grad = lax.psum_scatter(
        lax.dot_general(
            value_proj, value_grad, (((1,), (1,)), ((), ())), preferred_element_type=F32
        ),
        "dp",
        scatter_dimension=0,
        tiled=True,
    ).astype(BF16)
    return (steps.reshape(1, 2, PLANES * PEERS * ROWS, WIDTH), latent_grad)


def solution(mesh):
    in_specs = (
        P("expert", "dp"),
        P("expert", None),
        P("expert", None),
        P(),
        P("expert", None, None, None, "dp"),
        P(None, "expert", "dp"),
        P(None, "expert", "dp"),
        P("expert", "dp"),
        P(None, "dp"),
    )
    out_specs = (P("expert", None, None, "dp"), P("dp", "expert"))
    return jax.shard_map(shards, mesh=mesh, in_specs=in_specs, out_specs=out_specs, check_vma=False)
```

```python
import functools

import jax
import jax.numpy as jnp
from jax import lax
from jax.experimental import pallas as pl
from jax.experimental.pallas import tpu as pltpu
from jax.sharding import PartitionSpec as P

beta_first = 0.9
beta_second = 0.95
adam_eps = 1e-08
bias_first = 1.0 - 0.9**50 * 0.9**50
bias_second = 1.0 - 0.95**50 * 0.95**50

PLANES = 8
PEERS = 8
ROWS = 16
POS = 32
TOKENS = 640
FPART = 256
WIDTH = 896
CHUNKS = ((0, 256), (256, 256), (512, 256), (768, 128))
N = len(CHUNKS)
ORDER = (0, 1, -1, 2, -2, 3, -3, 4)
GROUPS = ((0, 3), (3, 5), (5, 8))
HALF = TOKENS // 2
TURNS = (1, 7, 2, 6, 3, 5, 4)
MESH = pl.DeviceIdType.MESH
F32 = jnp.float32
BF16 = jnp.bfloat16


def kernel(
    og,
    routes,
    gates,
    hid,
    dup,
    m1,
    m2,
    vgrad,
    vproj,
    out,
    latent,
    *refs,
):
    relay_x, relay_s, refs = refs[:N], refs[N : 2 * N], refs[2 * N :]
    tok, refs = refs[:N], refs[N:]
    rows_in, refs = refs[:N], refs[N:]
    grad_in, refs = refs[:N], refs[N:]
    rows_out, refs = refs[:N], refs[N:]
    (
        metas,
        gate_rows,
        onehot,
        gate_col,
        hid_t,
        part_out,
        step_out,
        mom,
        kron,
        kron_t,
        earlier,
        vg,
        vp,
        lat_part,
        lat_in,
        sem_meta,
        sem_ring,
        sem_ring_sent,
        sem_hid,
        sem_rows,
        sem_px,
        sem_pz,
        sem_sz,
        sem_last,
        sem_sx,
        sem_lat,
        sem_local,
        sem_own,
    ) = refs
    me = lax.axis_index("expert")
    y = lax.axis_index("dp")
    z = me // PEERS
    p = me % PEERS

    def plane(d):
        return lax.rem(z + d + PLANES, PLANES)

    def peer(d):
        return lax.rem(p + d + PEERS, PEERS)

    def dev_z(to):
        return {"expert": to * PEERS + p}

    def dev_p(to):
        return {"expert": z * PEERS + to}

    def dev_y(d):
        return {"dp": lax.rem(y + d + 4, 4)}

    def remote(src, dst, sent, arrived, device):
        return pltpu.make_async_remote_copy(
            src_ref=src,
            dst_ref=dst,
            send_sem=sent,
            recv_sem=arrived,
            device_id=device,
            device_id_type=MESH,
        )

    def all_sent(view, sem):
        remote(view, view, sem, sem, dev_p(p)).wait_send()

    def all_arrived(view, sem):
        remote(view, view, sem, sem, dev_p(p)).wait_recv()

    def others(body):
        def step(i, carry):
            body(i)
            return carry

        lax.fori_loop(1, 8, step, 0)

    def planes_in_turn(body):
        for i in TURNS:
            body(i)

    barrier = pltpu.get_barrier_semaphore()

    def greet(i):
        pl.semaphore_signal(barrier, inc=1, device_id=dev_z(plane(i)), device_id_type=MESH)
        pl.semaphore_signal(barrier, inc=1, device_id=dev_p(peer(i)), device_id_type=MESH)

    others(greet)
    for d in (1, 2, 3):
        pl.semaphore_signal(barrier, inc=1, device_id=dev_y(d), device_id_type=MESH)

    def local(src, dst, index):
        return pltpu.make_async_copy(src, dst, sem_local.at[index])

    own_tok = [
        local(og.at[:, pl.ds(CHUNKS[k][0], CHUNKS[k][1])], tok[k].at[z], k) for k in range(N)
    ]
    load_hid = [
        local(hid.at[plane(d)], rows_out[1].at[:, :, i], N + 6) for i, d in enumerate(ORDER)
    ]
    load_latent = [local(vgrad, vg, N), local(vproj, vp, N + 7)]
    load_meta = [local(routes, metas.at[z], N + 1), local(gates, gate_rows.at[z], N + 8)]

    def load_moments(k):
        c0, dc = CHUNKS[k]
        return [
            local(
                m.at[:, pl.ds(c0, dc)],
                mom.at[k % 2, i, :, pl.ds(0, dc)],
                N + 2 + 2 * (k % 2) + i,
            )
            for i, m in enumerate((m1, m2))
        ]

    for copy in load_hid + load_meta + own_tok[:1]:
        copy.start()

    with jax.named_scope("barrier"):
        pl.semaphore_wait(barrier, 17)

    def meta_copies(i):
        return [
            remote(source, into.at[z], sem_meta.at[0, j], sem_meta.at[1, j], dev_z(plane(i)))
            for j, (source, into) in enumerate(((routes, metas), (gates, gate_rows)))
        ]

    def send_meta(i):
        for copy in meta_copies(i):
            copy.start()

    def late_loads():
        for copy in own_tok[1:] + load_latent:
            copy.start()
        for k in (0, 1):
            for copy in load_moments(k):
                copy.start()

    def ring_send(k, way, step, half):
        c0, dc = CHUNKS[k]
        sign = 1 - 2 * way
        block = plane(-sign * (step - 1))
        rows = pl.ds(half * HALF, HALF)
        source = og.at[rows, pl.ds(c0, dc)] if step == 1 else tok[k].at[block, rows]
        arrived = sem_ring.at[k, way, step - 1, half]
        return remote(
            source, tok[k].at[block, rows], sem_ring_sent.at[k], arrived, dev_z(plane(sign))
        )

    def ring_arrival(k, way, step, half):
        sign = 1 - 2 * way
        block = plane(-sign * step)
        rows = pl.ds(half * HALF, HALF)
        arrived = sem_ring.at[k, way, step - 1, half]
        view = tok[k].at[block, rows]
        return remote(view, view, sem_ring_sent.at[k], arrived, dev_z(plane(sign)))

    def ring_parts(step):
        return [(way, half) for half in (0, 1) for way in (0, 1) if step < 4 or half == way]

    def ring_begin(k):
        for way, half in ring_parts(1):
            ring_send(k, way, 1, half).start()

    def ring_forward(k, step):
        for way, half in ring_parts(step):
            ring_arrival(k, way, step, half).wait_recv()
            if step < 3 or (step == 3 and half == way):
                ring_send(k, way, step + 1, half).start()

    def transpose_half(w):
        def piece(q, carry):
            hid_t[w, y, q] = rows_out[1][q, w].reshape(PLANES * POS, FPART).T
            return carry

        lax.fori_loop(0, PEERS, piece, 0)

    def y_part(d):
        return lax.rem(y + d + 4, 4)

    def hid_copy(index, w, part, d):
        view = hid_t.at[w, y_part(part)]
        return remote(view, view, sem_hid.at[6], sem_hid.at[index], dev_y(d))

    hid_copies = ((0, 0, 0, 1), (1, 1, 0, -1), (2, 1, 0, 1), (3, 0, 0, -1), (4, 0, -1, 1), (5, 1, 1, -1))

    def hid_send(index):
        hid_copy(*hid_copies[index]).start()

    def hid_wait(index):
        number, w, part, d = hid_copies[index]
        hid_copy(number, w, part - d, d).wait_recv()

    def build_plane(i):
        slot_of = lax.broadcasted_iota(jnp.int32, (16, TOKENS), 0) + z * 16
        named = jnp.zeros((16, TOKENS), F32)
        gate = jnp.zeros((16, TOKENS), F32)
        for k in range(4):
            match = slot_of == metas[i, k : k + 1, :]
            named = jnp.where(match, 1.0, named)
            gate = jnp.where(match, gate_rows[i, k : k + 1, :], gate)
        rank = jnp.dot(named.astype(BF16), earlier[...], preferred_element_type=F32)
        rank = jnp.where(named > 0.5, rank, -1.0)
        position = lax.broadcasted_iota(jnp.int32, (POS, TOKENS), 0).astype(F32)
        for s in range(16):
            chosen = position == rank[s : s + 1, :]
            onehot[i, s * POS : (s + 1) * POS, :] = jnp.where(chosen, 1.0, 0.0).astype(BF16)
            weight = jnp.sum(
                jnp.where(chosen, gate[s : s + 1, :], 0.0), axis=1, keepdims=True
            )
            gate_col[i, s * POS : (s + 1) * POS, :] = jnp.broadcast_to(weight, (POS, 128))

    def build(*distances):
        for d in distances:
            build_plane(plane(d))

    def gather(k, d):
        dc = CHUNKS[k][1]
        source, place = plane(d), ORDER.index(d)
        picked = jnp.dot(onehot[source], tok[k][source], preferred_element_type=F32)
        for part in range(dc // 128):
            lanes = slice(part * 128, (part + 1) * 128)
            scaled = (picked[:, lanes] * gate_col[source]).astype(BF16)
            rows_out[k][:, :, place, :, lanes] = scaled.reshape(PEERS, 2, POS, 128)

    def rows_copy(k, group, to):
        low, high = GROUPS[group]
        return remote(
            rows_out[k].at[to, :, low:high],
            rows_in[k].at[:, p, low:high],
            sem_rows.at[0, k],
            sem_rows.at[1, k],
            dev_p(to),
        )

    def own(src, dst, stage, k):
        return pltpu.make_async_copy(src, dst, sem_own.at[stage, k])

    def rows_own(k):
        return own(rows_out[k].at[p], rows_in[k].at[:, p], 0, k)

    def pick(k, *distances):
        for d in distances:
            gather(k, d)

    def send_rows(k, group):
        others(lambda i: rows_copy(k, group, peer(i)).start())
        if group == len(GROUPS) - 1:
            rows_own(k).start()

    def lat_copy(d):
        return remote(
            lat_part.at[y_part(d)], lat_in.at[d - 1], sem_lat.at[0], sem_lat.at[1], dev_y(d)
        )

    def latent_begin():
        for copy in load_latent:
            copy.wait()
        for i in range(4):
            lat_part[i] = lax.dot_general(
                vp[i * 128 : (i + 1) * 128, :],
                vg[...],
                (((1,), (1,)), ((), ())),
                preferred_element_type=F32,
            )
        for d in (1, 2, 3):
            lat_copy(d).start()

    def latent_end():
        all_arrived(lat_in, sem_lat.at[1])
        total = lat_part[y] + lat_in[0] + lat_in[1] + lat_in[2]
        vp[0:128, 0:TOKENS] = total.astype(BF16)
        store = local(vp.at[pl.ds(0, 128), pl.ds(0, TOKENS)], latent, N + 7)
        store.start()
        store.wait()

    def part_view(k, to):
        return part_out.at[k % 2, to, :, :, :, pl.ds(0, CHUNKS[k][1])]

    def part_copy(k, to):
        return remote(
            part_view(k, to), relay_x[k].at[:, p], sem_px.at[0, k], sem_px.at[1, k], dev_p(to)
        )

    def part_sent(k):
        all_sent(part_out.at[k % 2, 0:7, :, :, :, pl.ds(0, CHUNKS[k][1])], sem_px.at[0, k])

    def part_own(k):
        return own(part_view(k, p), relay_x[k].at[:, p], 1, k)

    def stage_matmul(k):
        dc = CHUNKS[k][1]
        rows_own(k).wait()
        all_arrived(rows_in[k].at[:, 0:7], sem_rows.at[1, k])
        if k >= 2:
            part_sent(k - 2)

        def block(i, carry):
            w = lax.rem(i, 2)
            part = lax.rem(y + i // 2, 4)
            total = jnp.zeros((FPART, dc), F32)
            for q in range(PEERS):
                total += jnp.dot(
                    hid_t[w, part, q],
                    rows_in[k][w, q].reshape(PLANES * POS, dc),
                    preferred_element_type=F32,
                )
            rounded = total.astype(BF16).reshape(2, PEERS, ROWS, dc)
            for h in range(2):
                for q in range(PEERS):
                    part_out[k % 2, q, w, 2 * part + h, :, 0:dc] = rounded[h, q]
            return carry

        lax.fori_loop(0, 8, block, 0)
        part_own(k).start()
        others(lambda i: part_copy(k, peer(i)).start())

    def grad_copy(k, to):
        return remote(
            relay_x[k].at[:, :, to],
            grad_in[k].at[:, z],
            sem_pz.at[0, k],
            sem_pz.at[1, k],
            dev_z(to),
        )

    def grad_own(k):
        return own(relay_x[k].at[:, :, z], grad_in[k].at[:, z], 2, k)

    def stage_forward(k):
        part_own(k).wait()
        all_arrived(relay_x[k].at[:, 0:7], sem_px.at[1, k])
        planes_in_turn(lambda i: grad_copy(k, plane(i)).start())
        grad_own(k).start()

    def step_view(k, to):
        return step_out.at[k % 2, :, to, :, :, pl.ds(0, CHUNKS[k][1])]

    def step_copy(k, to, index):
        arrived = sem_sz.at[1, k] if k < N - 2 else sem_last.at[k - (N - 2), index]
        return remote(step_view(k, to), relay_s[k].at[:, z], sem_sz.at[0, k], arrived, dev_z(to))

    def step_sent(k):
        all_sent(step_out.at[k % 2, :, 0:7, :, :, pl.ds(0, CHUNKS[k][1])], sem_sz.at[0, k])

    def step_own(k):
        return own(step_view(k, z), relay_s[k].at[:, z], 3, k)

    tile = 256
    per_tile = tile // (PEERS * ROWS)

    def stage_adam(k):
        dc = CHUNKS[k][1]
        grad_own(k).wait()
        all_arrived(grad_in[k].at[:, 0:7], sem_pz.at[1, k])
        if k >= 2:
            step_sent(k - 2)
        for copy in load_moments(k):
            copy.wait()

        def block(i, carry):
            rows = pl.ds(pl.multiple_of(i * tile, tile), tile)
            planes = pl.ds(i * per_tile, per_tile)
            twins = grad_in[k][1].reshape(PLANES * PEERS * ROWS, dc)
            gradient = grad_in[k][0, planes].reshape(tile, dc).astype(F32)
            gradient += jnp.dot(kron[rows, :], twins, preferred_element_type=F32)
            first = beta_first * mom[k % 2, 0, rows, 0:dc].astype(F32)
            first += (1.0 - beta_first) * gradient
            second = beta_second * mom[k % 2, 1, rows, 0:dc].astype(F32)
            second += (1.0 - beta_second) * gradient * gradient
            value = first / bias_first / (jnp.sqrt(second / bias_second) + adam_eps)
            value = value.astype(BF16).reshape(per_tile, PEERS, ROWS, dc)
            step_out[k % 2, 0, planes, :, :, 0:dc] = value
            return carry

        lax.fori_loop(0, PLANES // per_tile, block, 0)

        def twin(i, carry):
            rows = pl.ds(pl.multiple_of(i * tile, tile), tile)
            planes = pl.ds(i * per_tile, per_tile)
            steps = step_out[k % 2, 0, :, :, :, 0:dc].reshape(PLANES * PEERS * ROWS, dc)
            value = jnp.dot(kron_t[rows, :], steps, preferred_element_type=F32)
            value = value.astype(BF16).reshape(per_tile, PEERS, ROWS, dc)
            step_out[k % 2, 1, planes, :, :, 0:dc] = value
            return carry

        lax.fori_loop(0, PLANES // per_tile, twin, 0)
        step_own(k).start()
        planes_in_turn(lambda i: step_copy(k, plane(i), i).start())
        if k + 2 < N:
            for copy in load_moments(k + 2):
                copy.start()

    def columns(k):
        return pl.ds(CHUNKS[k][0], CHUNKS[k][1])

    def out_copy(k, to):
        return remote(
            relay_s[k].at[:, :, to],
            out.at[:, :, p, :, columns(k)],
            sem_sx.at[0, k],
            sem_sx.at[1, k],
            dev_p(to),
        )

    def out_own(k):
        return own(relay_s[k].at[:, :, p], out.at[:, :, p, :, columns(k)], 4, k)

    def plane_copy(k, source, to):
        return remote(
            relay_s[k].at[:, source, to],
            out.at[:, source, p, :, columns(k)],
            sem_sx.at[0, k],
            sem_sx.at[1, k],
            dev_p(to),
        )

    def stage_return(k):
        step_own(k).wait()
        if k < N - 2:
            all_arrived(relay_s[k].at[:, 0:7], sem_sz.at[1, k])
            out_own(k).start()
            others(lambda i: out_copy(k, peer(i)).start())
            return
        others(lambda i: plane_copy(k, z, peer(i)).start())
        for index in TURNS:
            source = plane(-index)
            view = relay_s[k].at[:, source]
            remote(
                view, view, sem_sz.at[0, k], sem_last.at[k - (N - 2), index], dev_z(source)
            ).wait_recv()
            others(lambda i: plane_copy(k, source, peer(i)).start())
        out_own(k).start()

    def drain_start():
        all_sent(metas.at[0:7], sem_meta.at[0, 0])
        all_sent(gate_rows.at[0:7], sem_meta.at[0, 1])
        all_sent(hid_t.at[:, 0:3], sem_hid.at[6])
        all_sent(lat_in, sem_lat.at[0])
        for k in range(N):
            all_sent(tok[k].at[0:7], sem_ring_sent.at[k])
            all_sent(rows_out[k].at[0:7], sem_rows.at[0, k])

    def drain_parts():
        for k in (N - 2, N - 1):
            part_sent(k)
        for k in range(N):
            all_sent(relay_x[k].at[:, :, 0:7], sem_pz.at[0, k])

    def drain_out(k):
        all_sent(relay_s[k].at[:, :, 0:7], sem_sx.at[0, k])
        all_arrived(out.at[:, :, 0:7, :, columns(k)], sem_sx.at[1, k])
        out_own(k).wait()

    def build_kron():
        spread = lax.broadcasted_iota(jnp.int32, (PLANES * PEERS, 1024), 1) // ROWS
        spread = spread == lax.broadcasted_iota(jnp.int32, (PLANES * PEERS, 1024), 0)
        owners = jnp.broadcast_to(dup[...].astype(F32), (16, PLANES * PEERS)).astype(BF16)
        owners = jnp.dot(owners, spread.astype(F32).astype(BF16), preferred_element_type=F32)
        offset = lax.broadcasted_iota(jnp.int32, (1, 1024), 1) % ROWS
        target = owners[0:1, :].astype(jnp.int32) * ROWS + offset
        for i in range(PLANES):
            rows = lax.broadcasted_iota(jnp.int32, (128, 1024), 0) + i * 128
            kron[i * 128 : (i + 1) * 128, :] = (
                jnp.where(rows == target, 1.0, 0.0).astype(BF16)
            )
            column = jnp.broadcast_to(target[:, i * 128 : (i + 1) * 128].astype(F32), (128, 128)).T
            for j in range(PLANES):
                lanes = lax.broadcasted_iota(jnp.int32, (128, 128), 1) + j * 128
                kron_t[i * 128 : (i + 1) * 128, j * 128 : (j + 1) * 128] = jnp.where(
                    lanes.astype(F32) == column, 1.0, 0.0
                ).astype(BF16)

    def wait_hid():
        for copy in load_hid:
            copy.wait()

    def prepare():
        for copy in load_meta:
            copy.wait()
        earlier[...] = (
            lax.broadcasted_iota(jnp.int32, (TOKENS, TOKENS), 0)
            < lax.broadcasted_iota(jnp.int32, (TOKENS, TOKENS), 1)
        ).astype(F32).astype(BF16)

    def meta_arrivals():
        all_arrived(metas.at[0:7], sem_meta.at[1, 0])
        all_arrived(gate_rows.at[0:7], sem_meta.at[1, 1])

    def own_wait(k):
        own_tok[k].wait()

    def hid_pass():
        hid_wait(0)
        hid_send(4)
        hid_send(2)
        hid_wait(1)
        hid_send(5)
        hid_send(3)

    def hid_finish():
        for index in (2, 3, 4, 5):
            hid_wait(index)

    with jax.named_scope("others"):
        others(send_meta)
    with jax.named_scope("ring_begin0"):
        ring_begin(0)
    with jax.named_scope("ring_begin1"):
        ring_begin(1)
    with jax.named_scope("wait_hid"):
        wait_hid()
    with jax.named_scope("transpose_half0"):
        transpose_half(0)
    with jax.named_scope("hid_send0"):
        hid_send(0)
    with jax.named_scope("transpose_half1"):
        transpose_half(1)
    with jax.named_scope("hid_send1"):
        hid_send(1)
    with jax.named_scope("late_loads"):
        late_loads()
    with jax.named_scope("prepare"):
        prepare()
    with jax.named_scope("meta_arrivals"):
        meta_arrivals()
    with jax.named_scope("build0"):
        build(0)
    with jax.named_scope("own_wait0"):
        own_wait(0)
    with jax.named_scope("pick00"):
        pick(0, 0)
    with jax.named_scope("build11"):
        build(1, -1)
    with jax.named_scope("ring_forward01"):
        ring_forward(0, 1)
    with jax.named_scope("pick011"):
        pick(0, 1, -1)
    with jax.named_scope("send_rows00"):
        send_rows(0, 0)
    with jax.named_scope("build22"):
        build(2, -2)
    with jax.named_scope("own_wait1"):
        own_wait(1)
    with jax.named_scope("pick10"):
        pick(1, 0)
    with jax.named_scope("ring_forward11"):
        ring_forward(1, 1)
    with jax.named_scope("pick111"):
        pick(1, 1, -1)
    with jax.named_scope("send_rows10"):
        send_rows(1, 0)
    with jax.named_scope("ring_forward02"):
        ring_forward(0, 2)
    with jax.named_scope("pick022"):
        pick(0, 2, -2)
    with jax.named_scope("send_rows01"):
        send_rows(0, 1)
    with jax.named_scope("build33"):
        build(3, -3)
    with jax.named_scope("hid_pass"):
        hid_pass()
    with jax.named_scope("ring_forward12"):
        ring_forward(1, 2)
    with jax.named_scope("pick122"):
        pick(1, 2, -2)
    with jax.named_scope("send_rows11"):
        send_rows(1, 1)
    with jax.named_scope("build4"):
        build(4)
    with jax.named_scope("build_kron"):
        build_kron()
    with jax.named_scope("ring_forward03"):
        ring_forward(0, 3)
    with jax.named_scope("ring_begin2"):
        ring_begin(2)
    with jax.named_scope("pick033"):
        pick(0, 3, -3)
    with jax.named_scope("ring_forward13"):
        ring_forward(1, 3)
    with jax.named_scope("ring_begin3"):
        ring_begin(3)
    with jax.named_scope("pick133"):
        pick(1, 3, -3)
    with jax.named_scope("ring_forward04"):
        ring_forward(0, 4)
    with jax.named_scope("pick04"):
        pick(0, 4)
    with jax.named_scope("send_rows02"):
        send_rows(0, 2)
    with jax.named_scope("ring_forward21"):
        ring_forward(2, 1)
    with jax.named_scope("own_wait2"):
        own_wait(2)
    with jax.named_scope("pick2011"):
        pick(2, 0, 1, -1)
    with jax.named_scope("send_rows20"):
        send_rows(2, 0)
    with jax.named_scope("ring_forward14"):
        ring_forward(1, 4)
    with jax.named_scope("pick14"):
        pick(1, 4)
    with jax.named_scope("send_rows12"):
        send_rows(1, 2)
    with jax.named_scope("ring_forward31"):
        ring_forward(3, 1)
    with jax.named_scope("own_wait3"):
        own_wait(3)
    with jax.named_scope("pick3011"):
        pick(3, 0, 1, -1)
    with jax.named_scope("ring_forward22"):
        ring_forward(2, 2)
    with jax.named_scope("pick222"):
        pick(2, 2, -2)
    with jax.named_scope("hid_finish"):
        hid_finish()
    with jax.named_scope("matmul0"):
        stage_matmul(0)
    with jax.named_scope("ring_forward32"):
        ring_forward(3, 2)
    with jax.named_scope("pick322"):
        pick(3, 2, -2)
    with jax.named_scope("matmul1"):
        stage_matmul(1)
    with jax.named_scope("ring_forward23"):
        ring_forward(2, 3)
    with jax.named_scope("pick233"):
        pick(2, 3, -3)
    with jax.named_scope("send_rows21"):
        send_rows(2, 1)
    with jax.named_scope("send_rows30"):
        send_rows(3, 0)
    with jax.named_scope("ring_forward33"):
        ring_forward(3, 3)
    with jax.named_scope("pick333"):
        pick(3, 3, -3)
    with jax.named_scope("forward0"):
        stage_forward(0)
    with jax.named_scope("ring_forward24"):
        ring_forward(2, 4)
    with jax.named_scope("pick24"):
        pick(2, 4)
    with jax.named_scope("send_rows22"):
        send_rows(2, 2)
    with jax.named_scope("send_rows31"):
        send_rows(3, 1)
    with jax.named_scope("ring_forward34"):
        ring_forward(3, 4)
    with jax.named_scope("pick34"):
        pick(3, 4)
    with jax.named_scope("send_rows32"):
        send_rows(3, 2)
    with jax.named_scope("forward1"):
        stage_forward(1)
    with jax.named_scope("latent_begin"):
        latent_begin()
    with jax.named_scope("matmul2"):
        stage_matmul(2)
    with jax.named_scope("matmul3"):
        stage_matmul(3)
    with jax.named_scope("adam0"):
        stage_adam(0)
    with jax.named_scope("forward2"):
        stage_forward(2)
    with jax.named_scope("forward3"):
        stage_forward(3)
    with jax.named_scope("adam1"):
        stage_adam(1)
    with jax.named_scope("return0"):
        stage_return(0)
    with jax.named_scope("latent_end"):
        latent_end()
    with jax.named_scope("adam2"):
        stage_adam(2)
    with jax.named_scope("drain_start"):
        drain_start()
    with jax.named_scope("return1"):
        stage_return(1)
    with jax.named_scope("adam3"):
        stage_adam(3)
    with jax.named_scope("drain_parts"):
        drain_parts()
    with jax.named_scope("return2"):
        stage_return(2)
    with jax.named_scope("drain_out0"):
        drain_out(0)
    with jax.named_scope("drain_out1"):
        drain_out(1)
    with jax.named_scope("step_sent2"):
        step_sent(2)
    with jax.named_scope("return3"):
        stage_return(3)
    with jax.named_scope("step_sent3"):
        step_sent(3)
    with jax.named_scope("drain_out2"):
        drain_out(2)
    with jax.named_scope("drain_out3"):
        drain_out(3)


def expert_steps(*operands):
    anywhere = pl.BlockSpec(memory_space=pl.ANY)
    relays = [
        jax.ShapeDtypeStruct((2, PEERS, PLANES, ROWS, dc), BF16) for _, dc in CHUNKS
    ]
    returns = [
        jax.ShapeDtypeStruct((2, PLANES, PEERS, ROWS, dc), BF16) for _, dc in CHUNKS
    ]
    shape = jax.ShapeDtypeStruct((2, PLANES, PEERS, ROWS, WIDTH), BF16)
    widest = max(dc for _, dc in CHUNKS)
    dma = pltpu.SemaphoreType.DMA
    scratch = [pltpu.VMEM((PLANES, TOKENS, dc), BF16) for _, dc in CHUNKS]
    scratch += [pltpu.VMEM((2, PEERS, PLANES, POS, dc), BF16) for _, dc in CHUNKS]
    scratch += [pltpu.VMEM((2, PLANES, PEERS, ROWS, dc), BF16) for _, dc in CHUNKS]
    scratch += [pltpu.VMEM((PEERS, 2, PLANES, POS, dc), BF16) for _, dc in CHUNKS]
    scratch += [
        pltpu.VMEM((PLANES, 4, TOKENS), jnp.int32),
        pltpu.VMEM((PLANES, 4, TOKENS), F32),
        pltpu.VMEM((PLANES, 16 * POS, TOKENS), BF16),
        pltpu.VMEM((PLANES, 16 * POS, 128), F32),
        pltpu.VMEM((2, 4, PEERS, FPART, PLANES * POS), BF16),
        pltpu.VMEM((2, PEERS, 2, PLANES, ROWS, widest), BF16),
        pltpu.VMEM((2, 2, PLANES, PEERS, ROWS, widest), BF16),
        pltpu.VMEM((2, 2, PLANES * PEERS * ROWS, widest), BF16),
        pltpu.VMEM((1024, 1024), BF16),
        pltpu.VMEM((1024, 1024), BF16),
        pltpu.VMEM((TOKENS, TOKENS), BF16),
        pltpu.VMEM((TOKENS, 1024), BF16),
        pltpu.VMEM((512, 1024), BF16),
        pltpu.VMEM((4, 128, TOKENS), F32),
        pltpu.VMEM((3, 128, TOKENS), F32),
        dma((2, 2)),
        dma((N, 2, 4, 2)),
        dma((N,)),
        dma((7,)),
        dma((2, N)),
        dma((2, N)),
        dma((2, N)),
        dma((2, N)),
        dma((2, 8)),
        dma((2, N)),
        dma((2,)),
        dma((N + 9,)),
        dma((5, N)),
    ]
    results = pl.pallas_call(
        kernel,
        out_shape=[shape, jax.ShapeDtypeStruct((128, TOKENS), BF16)] + relays + returns,
        in_specs=[anywhere] * 4 + [pl.BlockSpec(memory_space=pltpu.VMEM)] + [anywhere] * 4,
        out_specs=[anywhere] * (2 + 2 * N),
        scratch_shapes=scratch,
        compiler_params=pltpu.CompilerParams(
            collective_id=0, has_side_effects=True, vmem_limit_bytes=62 * 1024 * 1024
        ),
        cost_estimate=pl.CostEstimate(
            flops=50_000_000_000, bytes_accessed=60_000_000, transcendentals=2_000_000
        ),
    )(*operands)
    return results[0], results[1]


def shards(out_grad, routes, gates, dup_owner, hidden, moment1, moment2, value_grad, value_proj):
    experts = PLANES * PEERS
    hid = jnp.pad(hidden[0], ((0, 0), (0, 0), (0, POS - hidden.shape[3]), (0, 0)))
    hid = hid.reshape(PLANES, PEERS, 2, POS, FPART)
    steps, latent_grad = expert_steps(
        out_grad,
        routes.T,
        gates.T,
        hid,
        dup_owner.reshape(1, -1),
        moment1.reshape(experts * ROWS, WIDTH),
        moment2.reshape(experts * ROWS, WIDTH),
        value_grad,
        value_proj,
    )
    return (steps.reshape(1, 2, PLANES * PEERS * ROWS, WIDTH), latent_grad)


def solution(mesh):
    in_specs = (
        P("expert", "dp"),
        P("expert", None),
        P("expert", None),
        P(),
        P("expert", None, None, None, "dp"),
        P(None, "expert", "dp"),
        P(None, "expert", "dp"),
        P("expert", "dp"),
        P(None, "dp"),
    )
    out_specs = (P("expert", None, None, "dp"), P("dp", "expert"))
    return jax.shard_map(shards, mesh=mesh, in_specs=in_specs, out_specs=out_specs, check_vma=False)
```

```python
import functools

import jax
import jax.numpy as jnp
from jax import lax
from jax.experimental import pallas as pl
from jax.experimental.pallas import tpu as pltpu
from jax.sharding import PartitionSpec as P

beta_first = 0.9
beta_second = 0.95
adam_eps = 1e-08
bias_first = 1.0 - 0.9**50 * 0.9**50
bias_second = 1.0 - 0.95**50 * 0.95**50

PLANES = 8
PEERS = 8
ROWS = 16
CAP = 30
POS = 32
TOKENS = 640
FPART = 256
WIDTH = 896
CHUNKS = ((0, 256), (256, 256), (512, 256), (768, 128))
N = len(CHUNKS)
ORDER = (0, 1, -1, 2, -2, 3, -3, 4)
GROUPS = ((0, 3), (3, 5), (5, 8))
HALF = TOKENS // 2
TURNS = (1, 7, 2, 6, 3, 5, 4)
MESH = pl.DeviceIdType.MESH
F32 = jnp.float32
BF16 = jnp.bfloat16


def kernel(
    og,
    routes,
    gates,
    hid,
    dup,
    m1,
    m2,
    vgrad,
    vproj,
    out,
    latent,
    *refs,
):
    relay_x, relay_s, refs = refs[:N], list(refs[N : 2 * N - 2]), refs[2 * N - 2 :]
    tok, refs = refs[:N], refs[N:]
    rows_in, refs = refs[:N], refs[N:]
    grad_in, refs = refs[:N], refs[N:]
    rows_out, refs = refs[:N], refs[N:]
    relay_s, refs = relay_s + list(refs[:2]), refs[2:]
    (
        metas,
        gate_rows,
        onehot,
        gate_col,
        hid_t,
        part_out,
        step_out,
        mom,
        kron,
        kron_t,
        earlier,
        hid_raw,
        vg,
        vp,
        lat_part,
        lat_in,
        sem_meta,
        sem_ring,
        sem_ring_sent,
        sem_hid,
        sem_rows,
        sem_px,
        sem_pz,
        sem_sz,
        sem_last,
        sem_sx,
        sem_lat,
        sem_local,
        sem_own,
    ) = refs
    me = lax.axis_index("expert")
    y = lax.axis_index("dp")
    z = me // PEERS
    p = me % PEERS

    def plane(d):
        return lax.rem(z + d + PLANES, PLANES)

    def peer(d):
        return lax.rem(p + d + PEERS, PEERS)

    def dev_z(to):
        return {"expert": to * PEERS + p}

    def dev_p(to):
        return {"expert": z * PEERS + to}

    def dev_y(d):
        return {"dp": lax.rem(y + d + 4, 4)}

    def remote(src, dst, sent, arrived, device):
        return pltpu.make_async_remote_copy(
            src_ref=src,
            dst_ref=dst,
            send_sem=sent,
            recv_sem=arrived,
            device_id=device,
            device_id_type=MESH,
        )

    def all_sent(view, sem):
        remote(view, view, sem, sem, dev_p(p)).wait_send()

    def all_arrived(view, sem):
        remote(view, view, sem, sem, dev_p(p)).wait_recv()

    def others(body):
        def step(i, carry):
            body(i)
            return carry

        lax.fori_loop(1, 8, step, 0)

    def planes_in_turn(body):
        for i in TURNS:
            body(i)

    barrier = pltpu.get_barrier_semaphore()

    def greet(i):
        pl.semaphore_signal(barrier, inc=1, device_id=dev_z(plane(i)), device_id_type=MESH)
        pl.semaphore_signal(barrier, inc=1, device_id=dev_p(peer(i)), device_id_type=MESH)

    others(greet)
    for d in (1, 2, 3):
        pl.semaphore_signal(barrier, inc=1, device_id=dev_y(d), device_id_type=MESH)

    def local(src, dst, index):
        return pltpu.make_async_copy(src, dst, sem_local.at[index])

    own_tok = [
        local(og.at[:, pl.ds(CHUNKS[k][0], CHUNKS[k][1])], tok[k].at[z], k) for k in range(N)
    ]
    load_hid = [local(hid, hid_raw, N + 6)]
    load_latent = [local(vgrad, vg, N), local(vproj, vp, N + 7)]
    load_meta = [local(routes, metas.at[z], N + 1), local(gates, gate_rows.at[z], N + 8)]

    def load_moments(k):
        c0, dc = CHUNKS[k]
        return [
            local(
                m.at[:, pl.ds(c0, dc)],
                mom.at[k % 2, i, :, pl.ds(0, dc)],
                N + 2 + 2 * (k % 2) + i,
            )
            for i, m in enumerate((m1, m2))
        ]

    for copy in load_hid + load_meta + own_tok[:1]:
        copy.start()

    pl.semaphore_wait(barrier, 17)

    def meta_copies(i):
        return [
            remote(source, into.at[z], sem_meta.at[0, j], sem_meta.at[1, j], dev_z(plane(i)))
            for j, (source, into) in enumerate(((routes, metas), (gates, gate_rows)))
        ]

    def send_meta(i):
        for copy in meta_copies(i):
            copy.start()

    def late_loads():
        for copy in own_tok[1:] + load_latent:
            copy.start()
        for k in (0, 1):
            for copy in load_moments(k):
                copy.start()

    def ring_send(k, way, step, half):
        c0, dc = CHUNKS[k]
        sign = 1 - 2 * way
        block = plane(-sign * (step - 1))
        rows = pl.ds(half * HALF, HALF)
        source = og.at[rows, pl.ds(c0, dc)] if step == 1 else tok[k].at[block, rows]
        arrived = sem_ring.at[k, way, step - 1, half]
        return remote(
            source, tok[k].at[block, rows], sem_ring_sent.at[k], arrived, dev_z(plane(sign))
        )

    def ring_arrival(k, way, step, half):
        sign = 1 - 2 * way
        block = plane(-sign * step)
        rows = pl.ds(half * HALF, HALF)
        arrived = sem_ring.at[k, way, step - 1, half]
        view = tok[k].at[block, rows]
        return remote(view, view, sem_ring_sent.at[k], arrived, dev_z(plane(sign)))

    def ring_parts(step):
        return [(way, half) for half in (0, 1) for way in (0, 1) if step < 4 or half == way]

    def ring_begin(k):
        for way, half in ring_parts(1):
            ring_send(k, way, 1, half).start()

    def ring_forward(k, step):
        for way, half in ring_parts(step):
            ring_arrival(k, way, step, half).wait_recv()
            if step < 3 or (step == 3 and half == way):
                ring_send(k, way, step + 1, half).start()

    def transpose_half(w):
        def piece(q, carry):
            empty = jnp.zeros((POS - CAP, FPART), BF16)
            for i, d in enumerate(ORDER):
                rows_out[1][q, w, i, 0:CAP] = hid_raw[plane(d) * PEERS + q, :, w, :]
                rows_out[1][q, w, i, CAP:POS] = empty
            hid_t[w, y, q] = rows_out[1][q, w].reshape(PLANES * POS, FPART).T
            return carry

        lax.fori_loop(0, PEERS, piece, 0)

    def y_part(d):
        return lax.rem(y + d + 4, 4)

    def hid_copy(index, w, part, d):
        view = hid_t.at[w, y_part(part)]
        return remote(view, view, sem_hid.at[6], sem_hid.at[index], dev_y(d))

    hid_copies = (
        (0, 0, 0, 1),
        (1, 1, 0, -1),
        (2, 1, 0, 1),
        (3, 0, 0, -1),
        (4, 0, -1, 1),
        (5, 1, 1, -1),
    )

    def hid_send(index):
        hid_copy(*hid_copies[index]).start()

    def hid_wait(index):
        number, w, part, d = hid_copies[index]
        hid_copy(number, w, part - d, d).wait_recv()

    def build_plane(i):
        slot_of = lax.broadcasted_iota(jnp.int32, (16, TOKENS), 0) + z * 16
        named = jnp.zeros((16, TOKENS), F32)
        gate = jnp.zeros((16, TOKENS), F32)
        for k in range(4):
            match = slot_of == metas[i, k : k + 1, :]
            named = jnp.where(match, 1.0, named)
            gate = jnp.where(match, gate_rows[i, k : k + 1, :], gate)
        rank = jnp.dot(named.astype(BF16), earlier[...], preferred_element_type=F32)
        rank = jnp.where(named > 0.5, rank, -1.0)
        position = lax.broadcasted_iota(jnp.int32, (POS, TOKENS), 0).astype(F32)
        for s in range(16):
            chosen = position == rank[s : s + 1, :]
            onehot[i, s * POS : (s + 1) * POS, :] = jnp.where(chosen, 1.0, 0.0).astype(BF16)
            weight = jnp.sum(
                jnp.where(chosen, gate[s : s + 1, :], 0.0), axis=1, keepdims=True
            )
            gate_col[i, s * POS : (s + 1) * POS, :] = jnp.broadcast_to(weight, (POS, 128))

    def build(*distances):
        for d in distances:
            build_plane(plane(d))

    def gather(k, d):
        dc = CHUNKS[k][1]
        source, place = plane(d), ORDER.index(d)
        picked = jnp.dot(onehot[source], tok[k][source], preferred_element_type=F32)
        for part in range(dc // 128):
            lanes = slice(part * 128, (part + 1) * 128)
            scaled = (picked[:, lanes] * gate_col[source]).astype(BF16)
            rows_out[k][:, :, place, :, lanes] = scaled.reshape(PEERS, 2, POS, 128)

    def rows_copy(k, group, to):
        low, high = GROUPS[group]
        return remote(
            rows_out[k].at[to, :, low:high],
            rows_in[k].at[:, p, low:high],
            sem_rows.at[0, k],
            sem_rows.at[1, k],
            dev_p(to),
        )

    def own(src, dst, stage, k):
        return pltpu.make_async_copy(src, dst, sem_own.at[stage, k])

    def rows_own(k):
        return own(rows_out[k].at[p], rows_in[k].at[:, p], 0, k)

    def pick(k, *distances):
        for d in distances:
            gather(k, d)

    def send_rows(k, group):
        others(lambda i: rows_copy(k, group, peer(i)).start())
        if group == len(GROUPS) - 1:
            rows_own(k).start()

    def lat_copy(d):
        return remote(
            lat_part.at[y_part(d)], lat_in.at[d - 1], sem_lat.at[0], sem_lat.at[1], dev_y(d)
        )

    def latent_begin():
        for copy in load_latent:
            copy.wait()
        for i in range(4):
            lat_part[i] = lax.dot_general(
                vp[i * 128 : (i + 1) * 128, :],
                vg[...],
                (((1,), (1,)), ((), ())),
                preferred_element_type=F32,
            )
        for d in (1, 2, 3):
            lat_copy(d).start()

    def latent_end():
        all_arrived(lat_in, sem_lat.at[1])
        total = lat_part[y] + lat_in[0] + lat_in[1] + lat_in[2]
        vp[0:128, 0:TOKENS] = total.astype(BF16)
        store = local(vp.at[pl.ds(0, 128), pl.ds(0, TOKENS)], latent, N + 7)
        store.start()
        store.wait()

    def part_view(k, to):
        return part_out.at[k % 2, to, :, :, :, pl.ds(0, CHUNKS[k][1])]

    def part_copy(k, to):
        return remote(
            part_view(k, to), relay_x[k].at[:, p], sem_px.at[0, k], sem_px.at[1, k], dev_p(to)
        )

    def part_sent(k):
        all_sent(part_out.at[k % 2, 0:7, :, :, :, pl.ds(0, CHUNKS[k][1])], sem_px.at[0, k])

    def part_own(k):
        return own(part_view(k, p), relay_x[k].at[:, p], 1, k)

    def stage_matmul(k):
        dc = CHUNKS[k][1]
        rows_own(k).wait()
        all_arrived(rows_in[k].at[:, 0:7], sem_rows.at[1, k])
        if k >= 2:
            part_sent(k - 2)

        matmul(k, 0, 1, 2, 3)
        part_own(k).start()
        others(lambda i: part_copy(k, peer(i)).start())

    def matmul(k, *offsets):
        dc = CHUNKS[k][1]

        def block(i, carry):
            w = lax.rem(i, 2)
            part = y_part(offsets[0] + i // 2)
            total = jnp.zeros((FPART, dc), F32)
            for q in range(PEERS):
                total += jnp.dot(
                    hid_t[w, part, q],
                    rows_in[k][w, q].reshape(PLANES * POS, dc),
                    preferred_element_type=F32,
                )
            rounded = total.astype(BF16).reshape(2, PEERS, ROWS, dc)
            for h in range(2):
                for q in range(PEERS):
                    part_out[k % 2, q, w, 2 * part + h, :, 0:dc] = rounded[h, q]
            return carry

        lax.fori_loop(0, 2 * len(offsets), block, 0)

    def piece_sends(d):
        planes = pl.ds(2 * y_part(d), 2)

        def send(i):
            to = peer(i)
            remote(
                part_out.at[0, to, :, planes, :, pl.ds(0, CHUNKS[0][1])],
                relay_x[0].at[:, p, planes],
                sem_px.at[0, 0],
                sem_px.at[1, 0],
                dev_p(to),
            ).start()

        others(send)

    def matmul_near():
        rows_own(0).wait()
        all_arrived(rows_in[0].at[:, 0:7], sem_rows.at[1, 0])
        for d in (0, 1, -1):
            matmul(0, d)
            piece_sends(d)

    def matmul_far():
        matmul(0, 2)
        piece_sends(2)
        part_own(0).start()

    def grad_copy(k, to):
        return remote(
            relay_x[k].at[:, :, to],
            grad_in[k].at[:, z],
            sem_pz.at[0, k],
            sem_pz.at[1, k],
            dev_z(to),
        )

    def grad_own(k):
        return own(relay_x[k].at[:, :, z], grad_in[k].at[:, z], 2, k)

    def stage_forward(k):
        part_own(k).wait()
        all_arrived(relay_x[k].at[:, 0:7], sem_px.at[1, k])
        planes_in_turn(lambda i: grad_copy(k, plane(i)).start())
        grad_own(k).start()

    def step_view(k, to):
        return step_out.at[k % 2, :, to, :, :, pl.ds(0, CHUNKS[k][1])]

    def step_copy(k, to, index):
        arrived = sem_sz.at[1, k] if k < N - 2 else sem_last.at[k - (N - 2), index]
        return remote(step_view(k, to), relay_s[k].at[:, z], sem_sz.at[0, k], arrived, dev_z(to))

    def step_sent(k):
        all_sent(step_out.at[k % 2, :, 0:7, :, :, pl.ds(0, CHUNKS[k][1])], sem_sz.at[0, k])

    def step_own(k):
        return own(step_view(k, z), relay_s[k].at[:, z], 3, k)

    tile = 256
    per_tile = tile // (PEERS * ROWS)

    def stage_adam(k):
        dc = CHUNKS[k][1]
        grad_own(k).wait()
        all_arrived(grad_in[k].at[:, 0:7], sem_pz.at[1, k])
        if k >= 2:
            step_sent(k - 2)
        for copy in load_moments(k):
            copy.wait()

        def block(i, carry):
            rows = pl.ds(pl.multiple_of(i * tile, tile), tile)
            planes = pl.ds(i * per_tile, per_tile)
            twins = grad_in[k][1].reshape(PLANES * PEERS * ROWS, dc)
            gradient = grad_in[k][0, planes].reshape(tile, dc).astype(F32)
            gradient += jnp.dot(kron[rows, :], twins, preferred_element_type=F32)
            first = beta_first * mom[k % 2, 0, rows, 0:dc].astype(F32)
            first += (1.0 - beta_first) * gradient
            second = beta_second * mom[k % 2, 1, rows, 0:dc].astype(F32)
            second += (1.0 - beta_second) * gradient * gradient
            value = first / bias_first / (jnp.sqrt(second / bias_second) + adam_eps)
            value = value.astype(BF16).reshape(per_tile, PEERS, ROWS, dc)
            step_out[k % 2, 0, planes, :, :, 0:dc] = value
            return carry

        lax.fori_loop(0, PLANES // per_tile, block, 0)

        def twin(i, carry):
            rows = pl.ds(pl.multiple_of(i * tile, tile), tile)
            planes = pl.ds(i * per_tile, per_tile)
            steps = step_out[k % 2, 0, :, :, :, 0:dc].reshape(PLANES * PEERS * ROWS, dc)
            value = jnp.dot(kron_t[rows, :], steps, preferred_element_type=F32)
            value = value.astype(BF16).reshape(per_tile, PEERS, ROWS, dc)
            step_out[k % 2, 1, planes, :, :, 0:dc] = value
            return carry

        lax.fori_loop(0, PLANES // per_tile, twin, 0)
        step_own(k).start()
        planes_in_turn(lambda i: step_copy(k, plane(i), i).start())
        if k + 2 < N:
            for copy in load_moments(k + 2):
                copy.start()

    def columns(k):
        return pl.ds(CHUNKS[k][0], CHUNKS[k][1])

    def out_copy(k, to):
        return remote(
            relay_s[k].at[:, :, to],
            out.at[:, :, p, :, columns(k)],
            sem_sx.at[0, k],
            sem_sx.at[1, k],
            dev_p(to),
        )

    def out_own(k):
        return own(relay_s[k].at[:, :, p], out.at[:, :, p, :, columns(k)], 4, k)

    def plane_copy(k, source, to):
        return remote(
            relay_s[k].at[:, source, to],
            out.at[:, source, p, :, columns(k)],
            sem_sx.at[0, k],
            sem_sx.at[1, k],
            dev_p(to),
        )

    def plane_own(k, source):
        return own(relay_s[k].at[:, source, p], out.at[:, source, p, :, columns(k)], 4, k)

    def stage_return(k):
        step_own(k).wait()
        if k < N - 2:
            all_arrived(relay_s[k].at[:, 0:7], sem_sz.at[1, k])
            out_own(k).start()
            others(lambda i: out_copy(k, peer(i)).start())
            return
        plane_own(k, z).start()
        others(lambda i: plane_copy(k, z, peer(i)).start())
        for index in TURNS:
            source = plane(-index)
            view = relay_s[k].at[:, source]
            remote(
                view, view, sem_sz.at[0, k], sem_last.at[k - (N - 2), index], dev_z(source)
            ).wait_recv()
            plane_own(k, source).start()
            others(lambda i: plane_copy(k, source, peer(i)).start())

    def drain_start():
        all_sent(metas.at[0:7], sem_meta.at[0, 0])
        all_sent(gate_rows.at[0:7], sem_meta.at[0, 1])
        all_sent(hid_t.at[:, 0:3], sem_hid.at[6])
        all_sent(lat_in, sem_lat.at[0])
        for k in range(N):
            all_sent(tok[k].at[0:7], sem_ring_sent.at[k])
            all_sent(rows_out[k].at[0:7], sem_rows.at[0, k])

    def drain_parts():
        for k in (N - 2, N - 1):
            part_sent(k)
        for k in range(N):
            all_sent(relay_x[k].at[:, :, 0:7], sem_pz.at[0, k])

    def drain_out(k):
        all_sent(relay_s[k].at[:, :, 0:7], sem_sx.at[0, k])
        all_arrived(out.at[:, :, 0:7, :, columns(k)], sem_sx.at[1, k])
        out_own(k).wait()

    def build_kron():
        spread = lax.broadcasted_iota(jnp.int32, (PLANES * PEERS, 1024), 1) // ROWS
        spread = spread == lax.broadcasted_iota(jnp.int32, (PLANES * PEERS, 1024), 0)
        owners = jnp.broadcast_to(dup[...].astype(F32), (16, PLANES * PEERS)).astype(BF16)
        owners = jnp.dot(owners, spread.astype(F32).astype(BF16), preferred_element_type=F32)
        offset = lax.broadcasted_iota(jnp.int32, (1, 1024), 1) % ROWS
        target = owners[0:1, :].astype(jnp.int32) * ROWS + offset
        for i in range(PLANES):
            rows = lax.broadcasted_iota(jnp.int32, (128, 1024), 0) + i * 128
            kron[i * 128 : (i + 1) * 128, :] = (
                jnp.where(rows == target, 1.0, 0.0).astype(BF16)
            )
            column = jnp.broadcast_to(target[:, i * 128 : (i + 1) * 128].astype(F32), (128, 128)).T
            for j in range(PLANES):
                lanes = lax.broadcasted_iota(jnp.int32, (128, 128), 1) + j * 128
                kron_t[i * 128 : (i + 1) * 128, j * 128 : (j + 1) * 128] = jnp.where(
                    lanes.astype(F32) == column, 1.0, 0.0
                ).astype(BF16)

    def wait_hid():
        for copy in load_hid:
            copy.wait()

    def prepare():
        for copy in load_meta:
            copy.wait()
        earlier[...] = (
            lax.broadcasted_iota(jnp.int32, (TOKENS, TOKENS), 0)
            < lax.broadcasted_iota(jnp.int32, (TOKENS, TOKENS), 1)
        ).astype(F32).astype(BF16)

    def meta_arrivals():
        all_arrived(metas.at[0:7], sem_meta.at[1, 0])
        all_arrived(gate_rows.at[0:7], sem_meta.at[1, 1])

    def own_wait(k):
        own_tok[k].wait()

    def hid_pass():
        hid_wait(0)
        hid_send(4)
        hid_wait(1)
        hid_send(5)

    def hid_near():
        hid_wait(2)
        hid_wait(3)

    def hid_far():
        hid_wait(4)
        hid_wait(5)

    others(send_meta)
    ring_begin(0)
    ring_begin(1)
    wait_hid()
    transpose_half(0)
    hid_send(0)
    hid_send(3)
    transpose_half(1)
    hid_send(1)
    hid_send(2)
    late_loads()
    prepare()
    meta_arrivals()
    build(0)
    own_wait(0)
    pick(0, 0)
    build(1, -1)
    ring_forward(0, 1)
    pick(0, 1, -1)
    send_rows(0, 0)
    build(2, -2)
    own_wait(1)
    pick(1, 0)
    ring_forward(1, 1)
    pick(1, 1, -1)
    send_rows(1, 0)
    ring_forward(0, 2)
    pick(0, 2, -2)
    send_rows(0, 1)
    build(3, -3)
    ring_forward(1, 2)
    pick(1, 2, -2)
    send_rows(1, 1)
    build(4)
    build_kron()
    ring_forward(0, 3)
    ring_begin(2)
    pick(0, 3, -3)
    ring_forward(1, 3)
    ring_begin(3)
    pick(1, 3, -3)
    hid_pass()
    ring_forward(0, 4)
    pick(0, 4)
    send_rows(0, 2)
    ring_forward(2, 1)
    own_wait(2)
    pick(2, 0, 1, -1)
    ring_forward(1, 4)
    pick(1, 4)
    ring_forward(3, 1)
    hid_near()
    matmul_near()
    send_rows(1, 2)
    ring_forward(2, 2)
    pick(2, 2, -2)
    ring_forward(3, 2)
    hid_far()
    matmul_far()
    own_wait(3)
    pick(3, 0, 1, -1)
    ring_forward(2, 3)
    stage_matmul(1)
    send_rows(2, 0)
    ring_forward(3, 3)
    stage_forward(0)
    pick(3, 2, -2)
    pick(2, 3, -3)
    send_rows(2, 1)
    send_rows(3, 0)
    pick(3, 3, -3)
    send_rows(3, 1)
    ring_forward(2, 4)
    pick(2, 4)
    send_rows(2, 2)
    ring_forward(3, 4)
    pick(3, 4)
    send_rows(3, 2)
    stage_forward(1)
    latent_begin()
    stage_adam(0)
    stage_matmul(2)
    stage_matmul(3)
    stage_forward(2)
    stage_forward(3)
    stage_adam(1)
    stage_return(0)
    latent_end()
    stage_adam(2)
    drain_start()
    stage_return(1)
    stage_adam(3)
    drain_parts()
    stage_return(2)
    drain_out(0)
    drain_out(1)
    step_sent(2)
    stage_return(3)
    step_sent(3)
    drain_out(2)
    drain_out(3)


def expert_steps(*operands):
    anywhere = pl.BlockSpec(memory_space=pl.ANY)
    relays = [
        jax.ShapeDtypeStruct((2, PEERS, PLANES, ROWS, dc), BF16) for _, dc in CHUNKS
    ]
    returns = [
        jax.ShapeDtypeStruct((2, PLANES, PEERS, ROWS, dc), BF16) for _, dc in CHUNKS[: N - 2]
    ]
    shape = jax.ShapeDtypeStruct((2, PLANES, PEERS, ROWS, WIDTH), BF16)
    widest = max(dc for _, dc in CHUNKS)
    dma = pltpu.SemaphoreType.DMA
    scratch = [pltpu.VMEM((PLANES, TOKENS, dc), BF16) for _, dc in CHUNKS]
    scratch += [pltpu.VMEM((2, PEERS, PLANES, POS, dc), BF16) for _, dc in CHUNKS]
    scratch += [pltpu.VMEM((2, PLANES, PEERS, ROWS, dc), BF16) for _, dc in CHUNKS]
    scratch += [pltpu.VMEM((PEERS, 2, PLANES, POS, dc), BF16) for _, dc in CHUNKS]
    scratch += [pltpu.VMEM((2, PLANES, PEERS, ROWS, dc), BF16) for _, dc in CHUNKS[N - 2 :]]
    scratch += [
        pltpu.VMEM((PLANES, 4, TOKENS), jnp.int32),
        pltpu.VMEM((PLANES, 4, TOKENS), F32),
        pltpu.VMEM((PLANES, 16 * POS, TOKENS), BF16),
        pltpu.VMEM((PLANES, 16 * POS, 128), F32),
        pltpu.VMEM((2, 4, PEERS, FPART, PLANES * POS), BF16),
        pltpu.VMEM((2, PEERS, 2, PLANES, ROWS, widest), BF16),
        pltpu.VMEM((2, 2, PLANES, PEERS, ROWS, widest), BF16),
        pltpu.VMEM((2, 2, PLANES * PEERS * ROWS, widest), BF16),
        pltpu.VMEM((1024, 1024), BF16),
        pltpu.VMEM((1024, 1024), BF16),
        pltpu.VMEM((TOKENS, TOKENS), BF16),
        pltpu.VMEM((PLANES * PEERS, CAP, 2, FPART), BF16),
        pltpu.VMEM((TOKENS, 1024), BF16),
        pltpu.VMEM((512, 1024), BF16),
        pltpu.VMEM((4, 128, TOKENS), F32),
        pltpu.VMEM((3, 128, TOKENS), F32),
        dma((2, 2)),
        dma((N, 2, 4, 2)),
        dma((N,)),
        dma((7,)),
        dma((2, N)),
        dma((2, N)),
        dma((2, N)),
        dma((2, N)),
        dma((2, 8)),
        dma((2, N)),
        dma((2,)),
        dma((N + 9,)),
        dma((5, N)),
    ]
    results = pl.pallas_call(
        kernel,
        out_shape=[shape, jax.ShapeDtypeStruct((128, TOKENS), BF16)] + relays + returns,
        in_specs=[anywhere] * 4 + [pl.BlockSpec(memory_space=pltpu.VMEM)] + [anywhere] * 4,
        out_specs=[anywhere] * (2 * N),
        scratch_shapes=scratch,
        compiler_params=pltpu.CompilerParams(
            collective_id=0, has_side_effects=True, vmem_limit_bytes=62 * 1024 * 1024
        ),
        cost_estimate=pl.CostEstimate(
            flops=50_000_000_000, bytes_accessed=60_000_000, transcendentals=2_000_000
        ),
    )(*operands)
    return results[0], results[1]


def hand_over_kernel(steps, latent, steps_out, latent_out, steps_held, latent_held, sem):
    pieces = [
        (steps.at[w, i], steps_held.at[w, i], steps_out.at[w, i])
        for w in range(2)
        for i in range(PLANES)
    ]
    pieces.append((latent, latent_held, latent_out))
    into = [
        pltpu.make_async_copy(a, b, sem.at[0, n]) for n, (a, b, _) in enumerate(pieces)
    ]
    back = [
        pltpu.make_async_copy(b, c, sem.at[1, n]) for n, (_, b, c) in enumerate(pieces)
    ]
    for copy in into:
        copy.start()
    for first, second in zip(into, back):
        first.wait()
        second.start()
    for copy in back:
        copy.wait()


def hand_over(*results):
    anywhere = pl.BlockSpec(memory_space=pl.ANY)
    return pl.pallas_call(
        hand_over_kernel,
        out_shape=[jax.ShapeDtypeStruct(r.shape, r.dtype) for r in results],
        in_specs=[anywhere] * 2,
        out_specs=[anywhere] * 2,
        scratch_shapes=[pltpu.VMEM(r.shape, r.dtype) for r in results]
        + [pltpu.SemaphoreType.DMA((2, 2 * PLANES + 1))],
    )(*results)


def shards(out_grad, routes, gates, dup_owner, hidden, moment1, moment2, value_grad, value_proj):
    experts = PLANES * PEERS
    hid = hidden[0].transpose(0, 2, 1, 3)
    steps, latent_grad = expert_steps(
        out_grad,
        routes.T,
        gates.T,
        hid,
        dup_owner.reshape(1, -1),
        moment1.reshape(experts * ROWS, WIDTH),
        moment2.reshape(experts * ROWS, WIDTH),
        value_grad,
        value_proj,
    )
    steps, latent_grad = hand_over(steps, latent_grad)
    return (steps.reshape(1, 2, PLANES * PEERS * ROWS, WIDTH), latent_grad)


def solution(mesh):
    in_specs = (
        P("expert", "dp"),
        P("expert", None),
        P("expert", None),
        P(),
        P("expert", None, None, None, "dp"),
        P(None, "expert", "dp"),
        P(None, "expert", "dp"),
        P("expert", "dp"),
        P(None, "dp"),
    )
    out_specs = (P("expert", None, None, "dp"), P("dp", "expert"))
    return jax.shard_map(shards, mesh=mesh, in_specs=in_specs, out_specs=out_specs, check_vma=False)
```

```python
import functools

import jax
import jax.numpy as jnp
from jax import lax
from jax.experimental import pallas as pl
from jax.experimental.pallas import tpu as pltpu
from jax.sharding import PartitionSpec as P

beta_first = 0.9
beta_second = 0.95
adam_eps = 1e-08
bias_first = 1.0 - 0.9**50 * 0.9**50
bias_second = 1.0 - 0.95**50 * 0.95**50

PLANES = 8
PEERS = 8
ROWS = 16
CAP = 30
POS = 32
TOKENS = 640
FPART = 256
WIDTH = 896
CHUNKS = ((0, 256), (256, 256), (512, 256), (768, 128))
N = len(CHUNKS)
ORDER = (0, 1, -1, 2, -2, 3, -3, 4)
GROUPS = ((0, 3), (3, 5), (5, 8))
HALF = TOKENS // 2
NEED = 16 * CAP
TURNS = (1, 7, 2, 6, 3, 5, 4)
MESH = pl.DeviceIdType.MESH
F32 = jnp.float32
BF16 = jnp.bfloat16


def kernel(
    og,
    routes,
    gates,
    hid,
    dup,
    m1,
    m2,
    vgrad,
    vproj,
    out,
    latent,
    *refs,
):
    relay_x, relay_s, refs = refs[:N], list(refs[N : 2 * N - 1]), refs[2 * N - 1 :]
    tok, refs = refs[:N], refs[N:]
    rows_in, refs = refs[:N], refs[N:]
    grad_in, refs = refs[:N], refs[N:]
    rows_out, refs = refs[:N], refs[N:]
    relay_s, refs = relay_s + list(refs[:1]), refs[1:]
    (
        metas,
        gate_rows,
        onehot,
        onehot_kept,
        gate_col,
        hid_t,
        part_out,
        step_out,
        mom,
        kron,
        kron_t,
        earlier,
        hid_raw,
        vg,
        vp,
        lat_part,
        lat_in,
        sem_meta,
        sem_ring,
        sem_ring_sent,
        sem_hid,
        sem_rows,
        sem_px,
        sem_pz,
        sem_sz,
        sem_last,
        sem_sx,
        sem_lat,
        sem_local,
        sem_own,
    ) = refs
    me = lax.axis_index("expert")
    y = lax.axis_index("dp")
    z = me // PEERS
    p = me % PEERS

    def plane(d):
        return lax.rem(z + d + PLANES, PLANES)

    def peer(d):
        return lax.rem(p + d + PEERS, PEERS)

    def dev_z(to):
        return {"expert": to * PEERS + p}

    def dev_p(to):
        return {"expert": z * PEERS + to}

    def dev_y(d):
        return {"dp": lax.rem(y + d + 4, 4)}

    def remote(src, dst, sent, arrived, device):
        return pltpu.make_async_remote_copy(
            src_ref=src,
            dst_ref=dst,
            send_sem=sent,
            recv_sem=arrived,
            device_id=device,
            device_id_type=MESH,
        )

    def all_sent(view, sem):
        remote(view, view, sem, sem, dev_p(p)).wait_send()

    def all_arrived(view, sem):
        remote(view, view, sem, sem, dev_p(p)).wait_recv()

    def others(body):
        def step(i, carry):
            body(i)
            return carry

        lax.fori_loop(1, 8, step, 0)

    def planes_in_turn(body):
        for i in TURNS:
            body(i)

    barrier = pltpu.get_barrier_semaphore()

    def greet(i):
        pl.semaphore_signal(barrier, inc=1, device_id=dev_z(plane(i)), device_id_type=MESH)
        pl.semaphore_signal(barrier, inc=1, device_id=dev_p(peer(i)), device_id_type=MESH)

    others(greet)
    for d in (1, 2, 3):
        pl.semaphore_signal(barrier, inc=1, device_id=dev_y(d), device_id_type=MESH)

    def local(src, dst, index):
        return pltpu.make_async_copy(src, dst, sem_local.at[index])

    own_tok = [
        local(og.at[:, pl.ds(CHUNKS[k][0], CHUNKS[k][1])], tok[k].at[z], k) for k in range(N)
    ]
    load_hid = [local(hid, hid_raw, N + 6)]
    load_latent = [local(vgrad, vg, N), local(vproj, vp, N + 7)]
    load_meta = [local(routes, metas.at[z], N + 1), local(gates, gate_rows.at[z], N + 8)]

    def load_moments(k):
        c0, dc = CHUNKS[k]
        return [
            local(
                m.at[:, pl.ds(c0, dc)],
                mom.at[k % 2, i, :, pl.ds(0, dc)],
                N + 2 + 2 * (k % 2) + i,
            )
            for i, m in enumerate((m1, m2))
        ]

    for copy in load_hid + load_meta + own_tok[:1]:
        copy.start()

    pl.semaphore_wait(barrier, 17)

    def meta_copies(i):
        return [
            remote(source, into.at[z], sem_meta.at[0, j], sem_meta.at[1, j], dev_z(plane(i)))
            for j, (source, into) in enumerate(((routes, metas), (gates, gate_rows)))
        ]

    def send_meta(i):
        for copy in meta_copies(i):
            copy.start()

    def late_loads():
        for copy in own_tok[1:] + load_latent:
            copy.start()
        for k in (0, 1):
            for copy in load_moments(k):
                copy.start()

    def last_step(k, way):
        return 4 if way == k % 2 else 3

    def ring_rows(k, way, step, half):
        size = HALF if step < last_step(k, way) else NEED // 2
        return pl.ds(half * size, size)

    def ring_sent(k, way, step):
        return sem_ring_sent.at[0 if step < last_step(k, way) else 1, k]

    def ring_send(k, way, step, half):
        c0, dc = CHUNKS[k]
        sign = 1 - 2 * way
        block = plane(-sign * (step - 1))
        rows = ring_rows(k, way, step, half)
        source = og.at[rows, pl.ds(c0, dc)] if step == 1 else tok[k].at[block, rows]
        arrived = sem_ring.at[k, way, step - 1, half]
        return remote(
            source, tok[k].at[block, rows], ring_sent(k, way, step), arrived, dev_z(plane(sign))
        )

    def ring_arrival(k, way, step, half):
        sign = 1 - 2 * way
        view = tok[k].at[plane(-sign * step), ring_rows(k, way, step, half)]
        arrived = sem_ring.at[k, way, step - 1, half]
        return remote(view, view, ring_sent(k, way, step), arrived, dev_z(plane(sign)))

    def ring_begin(k):
        for half in (0, 1):
            for way in (0, 1):
                ring_send(k, way, 1, half).start()

    def ring_forward(k, step):
        ways = [way for way in (0, 1) if step <= last_step(k, way)]
        for half in (0, 1):
            for way in ways:
                ring_arrival(k, way, step, half).wait_recv()
                if step + 1 < last_step(k, way):
                    ring_send(k, way, step + 1, half).start()
        for way in ways:
            if step + 1 == last_step(k, way):
                sign = 1 - 2 * way
                gather(k, -sign * step)
                block = plane(-sign * step)
                chosen = selection(needed(block, plane(sign)))
                kept = jnp.dot(chosen, tok[k][block], preferred_element_type=F32)
                tok[k][block, 0:NEED] = kept.astype(BF16)
                for half in (0, 1):
                    ring_send(k, way, step + 1, half).start()

    def needed(group, of_plane):
        match = jnp.where(lax.shift_right_logical(metas[group], 4) == of_plane, 1.0, 0.0)
        return jnp.max(match, axis=0, keepdims=True)

    def selection(need):
        before = jnp.dot(
            jnp.broadcast_to(need, (16, TOKENS)).astype(BF16),
            earlier[...],
            preferred_element_type=F32,
        )
        place = jnp.where(need > 0.5, before[0:1, :], -1.0)
        position = lax.broadcasted_iota(jnp.int32, (NEED, TOKENS), 0).astype(F32)
        return jnp.where(position == place, 1.0, 0.0).astype(BF16)

    def transpose_half(w):
        def piece(q, carry):
            empty = jnp.zeros((POS - CAP, FPART), BF16)
            for i, d in enumerate(ORDER):
                rows_out[1][q, w, i, 0:CAP] = hid_raw[plane(d) * PEERS + q, :, w, :]
                rows_out[1][q, w, i, CAP:POS] = empty
            hid_t[w, y, q] = rows_out[1][q, w].reshape(PLANES * POS, FPART).T
            return carry

        lax.fori_loop(0, PEERS, piece, 0)

    def y_part(d):
        return lax.rem(y + d + 4, 4)

    def hid_copy(index, w, part, d):
        view = hid_t.at[w, y_part(part)]
        return remote(view, view, sem_hid.at[6], sem_hid.at[index], dev_y(d))

    hid_copies = (
        (0, 0, 0, 1),
        (1, 1, 0, -1),
        (2, 1, 0, 1),
        (3, 0, 0, -1),
        (4, 0, -1, 1),
        (5, 1, 1, -1),
    )

    def hid_send(index):
        hid_copy(*hid_copies[index]).start()

    def hid_wait(index):
        number, w, part, d = hid_copies[index]
        hid_copy(number, w, part - d, d).wait_recv()

    def build_plane(d):
        i = plane(d)
        slot_of = lax.broadcasted_iota(jnp.int32, (16, TOKENS), 0) + z * 16
        named = jnp.zeros((16, TOKENS), F32)
        gate = jnp.zeros((16, TOKENS), F32)
        for k in range(4):
            match = slot_of == metas[i, k : k + 1, :]
            named = jnp.where(match, 1.0, named)
            gate = jnp.where(match, gate_rows[i, k : k + 1, :], gate)
        rank = jnp.dot(named.astype(BF16), earlier[...], preferred_element_type=F32)
        rank = jnp.where(named > 0.5, rank, -1.0)
        position = lax.broadcasted_iota(jnp.int32, (POS, TOKENS), 0).astype(F32)
        for s in range(16):
            chosen = position == rank[s : s + 1, :]
            onehot[i, s * POS : (s + 1) * POS, :] = jnp.where(chosen, 1.0, 0.0).astype(BF16)
            weight = jnp.sum(
                jnp.where(chosen, gate[s : s + 1, :], 0.0), axis=1, keepdims=True
            )
            gate_col[i, s * POS : (s + 1) * POS, :] = jnp.broadcast_to(weight, (POS, 128))
        if abs(d) >= 3:
            kept = lax.dot_general(
                (rank + 1.0).astype(BF16),
                selection(needed(i, z)),
                (((1,), (1,)), ((), ())),
                preferred_element_type=F32,
            )
            kept = kept - 1.0
            position = lax.broadcasted_iota(jnp.int32, (POS, NEED), 0).astype(F32)
            for s in range(16):
                chosen = jnp.where(position == kept[s : s + 1, :], 1.0, 0.0).astype(BF16)
                if d == 4:
                    onehot[i, s * POS : (s + 1) * POS, 0:NEED] = chosen
                else:
                    onehot_kept[(d + 3) // 6, s * POS : (s + 1) * POS, :] = chosen

    def build(*distances):
        for d in distances:
            build_plane(d)

    def gather(k, d):
        dc = CHUNKS[k][1]
        source, place = plane(d), ORDER.index(d)
        if d == 4:
            picks, rows = onehot[source, :, 0:NEED], tok[k][source, 0:NEED]
        elif d == (3 if k % 2 == 0 else -3):
            picks, rows = onehot_kept[(d + 3) // 6], tok[k][source, 0:NEED]
        else:
            picks, rows = onehot[source], tok[k][source]
        picked = jnp.dot(picks, rows, preferred_element_type=F32)
        for part in range(dc // 128):
            lanes = slice(part * 128, (part + 1) * 128)
            scaled = (picked[:, lanes] * gate_col[source]).astype(BF16)
            rows_out[k][:, :, place, :, lanes] = scaled.reshape(PEERS, 2, POS, 128)

    def rows_copy(k, group, to):
        low, high = GROUPS[group]
        return remote(
            rows_out[k].at[to, :, low:high],
            rows_in[k].at[:, p, low:high],
            sem_rows.at[0, k],
            sem_rows.at[1, k],
            dev_p(to),
        )

    def own(src, dst, stage, k):
        return pltpu.make_async_copy(src, dst, sem_own.at[stage, k])

    def rows_own(k):
        return own(rows_out[k].at[p], rows_in[k].at[:, p], 0, k)

    def pick(k, *distances):
        ahead = (-3, 2) if k % 2 == 0 else (3, -2)
        for d in distances:
            if d not in ahead:
                gather(k, d)

    def send_rows(k, group):
        others(lambda i: rows_copy(k, group, peer(i)).start())
        if group == len(GROUPS) - 1:
            rows_own(k).start()

    def lat_copy(d):
        return remote(
            lat_part.at[y_part(d)], lat_in.at[d - 1], sem_lat.at[0], sem_lat.at[1], dev_y(d)
        )

    def latent_begin():
        for copy in load_latent:
            copy.wait()
        for i in range(4):
            lat_part[i] = lax.dot_general(
                vp[i * 128 : (i + 1) * 128, :],
                vg[...],
                (((1,), (1,)), ((), ())),
                preferred_element_type=F32,
            )
        for d in (1, 2, 3):
            lat_copy(d).start()

    def latent_end():
        all_arrived(lat_in, sem_lat.at[1])
        total = lat_part[y] + lat_in[0] + lat_in[1] + lat_in[2]
        vp[0:128, 0:TOKENS] = total.astype(BF16)
        store = local(vp.at[pl.ds(0, 128), pl.ds(0, TOKENS)], latent, N + 7)
        store.start()
        store.wait()

    def part_view(k, to):
        return part_out.at[k % 2, to, :, :, :, pl.ds(0, CHUNKS[k][1])]

    def part_copy(k, to):
        return remote(
            part_view(k, to), relay_x[k].at[:, p], sem_px.at[0, k], sem_px.at[1, k], dev_p(to)
        )

    def part_sent(k):
        all_sent(part_out.at[k % 2, 0:7, :, :, :, pl.ds(0, CHUNKS[k][1])], sem_px.at[0, k])

    def part_own(k):
        return own(part_view(k, p), relay_x[k].at[:, p], 1, k)

    def stage_matmul(k):
        dc = CHUNKS[k][1]
        rows_own(k).wait()
        all_arrived(rows_in[k].at[:, 0:7], sem_rows.at[1, k])
        if k >= 2:
            part_sent(k - 2)

        matmul(k, 0, 1, 2, 3)
        part_own(k).start()
        others(lambda i: part_copy(k, peer(i)).start())

    def matmul(k, *offsets):
        dc = CHUNKS[k][1]

        def block(i, carry):
            w = lax.rem(i, 2)
            part = y_part(offsets[0] + i // 2)
            total = jnp.zeros((FPART, dc), F32)
            for q in range(PEERS):
                total += jnp.dot(
                    hid_t[w, part, q],
                    rows_in[k][w, q].reshape(PLANES * POS, dc),
                    preferred_element_type=F32,
                )
            rounded = total.astype(BF16).reshape(2, PEERS, ROWS, dc)
            for h in range(2):
                for q in range(PEERS):
                    part_out[k % 2, q, w, 2 * part + h, :, 0:dc] = rounded[h, q]
            return carry

        lax.fori_loop(0, 2 * len(offsets), block, 0)

    def piece_sends(d):
        planes = pl.ds(2 * y_part(d), 2)

        def send(i):
            to = peer(i)
            remote(
                part_out.at[0, to, :, planes, :, pl.ds(0, CHUNKS[0][1])],
                relay_x[0].at[:, p, planes],
                sem_px.at[0, 0],
                sem_px.at[1, 0],
                dev_p(to),
            ).start()

        others(send)

    def matmul_near():
        rows_own(0).wait()
        all_arrived(rows_in[0].at[:, 0:7], sem_rows.at[1, 0])
        for d in (0, 1, -1):
            matmul(0, d)
            piece_sends(d)

    def matmul_far():
        matmul(0, 2)
        piece_sends(2)
        part_own(0).start()

    def grad_copy(k, to):
        return remote(
            relay_x[k].at[:, :, to],
            grad_in[k].at[:, z],
            sem_pz.at[0, k],
            sem_pz.at[1, k],
            dev_z(to),
        )

    def grad_own(k):
        return own(relay_x[k].at[:, :, z], grad_in[k].at[:, z], 2, k)

    def stage_forward(k):
        part_own(k).wait()
        all_arrived(relay_x[k].at[:, 0:7], sem_px.at[1, k])
        planes_in_turn(lambda i: grad_copy(k, plane(i)).start())
        grad_own(k).start()

    def step_view(k, to):
        return step_out.at[k % 2, :, to, :, :, pl.ds(0, CHUNKS[k][1])]

    def step_copy(k, to, index):
        arrived = sem_sz.at[1, k] if k < N - 2 else sem_last.at[k - (N - 2), index]
        return remote(step_view(k, to), relay_s[k].at[:, z], sem_sz.at[0, k], arrived, dev_z(to))

    def step_sent(k):
        all_sent(step_out.at[k % 2, :, 0:7, :, :, pl.ds(0, CHUNKS[k][1])], sem_sz.at[0, k])

    def step_own(k):
        return own(step_view(k, z), relay_s[k].at[:, z], 3, k)

    tile = 256
    per_tile = tile // (PEERS * ROWS)

    def stage_adam(k):
        dc = CHUNKS[k][1]
        grad_own(k).wait()
        all_arrived(grad_in[k].at[:, 0:7], sem_pz.at[1, k])
        if k >= 2:
            step_sent(k - 2)
        for copy in load_moments(k):
            copy.wait()

        def block(i, carry):
            rows = pl.ds(pl.multiple_of(i * tile, tile), tile)
            planes = pl.ds(i * per_tile, per_tile)
            twins = grad_in[k][1].reshape(PLANES * PEERS * ROWS, dc)
            gradient = grad_in[k][0, planes].reshape(tile, dc).astype(F32)
            gradient += jnp.dot(kron[rows, :], twins, preferred_element_type=F32)
            first = beta_first * mom[k % 2, 0, rows, 0:dc].astype(F32)
            first += (1.0 - beta_first) * gradient
            second = beta_second * mom[k % 2, 1, rows, 0:dc].astype(F32)
            second += (1.0 - beta_second) * gradient * gradient
            value = first / bias_first / (jnp.sqrt(second / bias_second) + adam_eps)
            value = value.astype(BF16).reshape(per_tile, PEERS, ROWS, dc)
            step_out[k % 2, 0, planes, :, :, 0:dc] = value
            return carry

        lax.fori_loop(0, PLANES // per_tile, block, 0)

        def twin(i, carry):
            rows = pl.ds(pl.multiple_of(i * tile, tile), tile)
            planes = pl.ds(i * per_tile, per_tile)
            steps = step_out[k % 2, 0, :, :, :, 0:dc].reshape(PLANES * PEERS * ROWS, dc)
            value = jnp.dot(kron_t[rows, :], steps, preferred_element_type=F32)
            value = value.astype(BF16).reshape(per_tile, PEERS, ROWS, dc)
            step_out[k % 2, 1, planes, :, :, 0:dc] = value
            return carry

        lax.fori_loop(0, PLANES // per_tile, twin, 0)
        step_own(k).start()
        planes_in_turn(lambda i: step_copy(k, plane(i), i).start())
        if k + 2 < N:
            for copy in load_moments(k + 2):
                copy.start()

    def columns(k):
        return pl.ds(CHUNKS[k][0], CHUNKS[k][1])

    def out_copy(k, to):
        return remote(
            relay_s[k].at[:, :, to],
            out.at[:, :, p, :, columns(k)],
            sem_sx.at[0, k],
            sem_sx.at[1, k],
            dev_p(to),
        )

    def out_own(k):
        return own(relay_s[k].at[:, :, p], out.at[:, :, p, :, columns(k)], 4, k)

    def plane_copy(k, source, to):
        return remote(
            relay_s[k].at[:, source, to],
            out.at[:, source, p, :, columns(k)],
            sem_sx.at[0, k],
            sem_sx.at[1, k],
            dev_p(to),
        )

    def plane_own(k, source):
        return own(relay_s[k].at[:, source, p], out.at[:, source, p, :, columns(k)], 4, k)

    def stage_return(k):
        step_own(k).wait()
        if k < N - 2:
            all_arrived(relay_s[k].at[:, 0:7], sem_sz.at[1, k])
            out_own(k).start()
            others(lambda i: out_copy(k, peer(i)).start())
            return
        plane_own(k, z).start()
        others(lambda i: plane_copy(k, z, peer(i)).start())
        for index in TURNS:
            source = plane(-index)
            view = relay_s[k].at[:, source]
            remote(
                view, view, sem_sz.at[0, k], sem_last.at[k - (N - 2), index], dev_z(source)
            ).wait_recv()
            plane_own(k, source).start()
            others(lambda i: plane_copy(k, source, peer(i)).start())

    def drain_start():
        all_sent(metas.at[0:7], sem_meta.at[0, 0])
        all_sent(gate_rows.at[0:7], sem_meta.at[0, 1])
        all_sent(hid_t.at[:, 0:3], sem_hid.at[6])
        all_sent(lat_in, sem_lat.at[0])
        for k in range(N):
            all_sent(tok[k].at[0:5], sem_ring_sent.at[0, k])
            all_sent(tok[k].at[0:2, 0:NEED], sem_ring_sent.at[1, k])
            all_sent(rows_out[k].at[0:7], sem_rows.at[0, k])

    def drain_parts():
        for k in (N - 2, N - 1):
            part_sent(k)
        for k in range(N):
            all_sent(relay_x[k].at[:, :, 0:7], sem_pz.at[0, k])

    def drain_out(k):
        all_sent(relay_s[k].at[:, :, 0:7], sem_sx.at[0, k])
        all_arrived(out.at[:, :, 0:7, :, columns(k)], sem_sx.at[1, k])
        out_own(k).wait()

    def build_kron():
        spread = lax.broadcasted_iota(jnp.int32, (PLANES * PEERS, 1024), 1) // ROWS
        spread = spread == lax.broadcasted_iota(jnp.int32, (PLANES * PEERS, 1024), 0)
        owners = jnp.broadcast_to(dup[...].astype(F32), (16, PLANES * PEERS)).astype(BF16)
        owners = jnp.dot(owners, spread.astype(F32).astype(BF16), preferred_element_type=F32)
        offset = lax.broadcasted_iota(jnp.int32, (1, 1024), 1) % ROWS
        target = owners[0:1, :].astype(jnp.int32) * ROWS + offset
        for i in range(PLANES):
            rows = lax.broadcasted_iota(jnp.int32, (128, 1024), 0) + i * 128
            kron[i * 128 : (i + 1) * 128, :] = (
                jnp.where(rows == target, 1.0, 0.0).astype(BF16)
            )
            column = jnp.broadcast_to(target[:, i * 128 : (i + 1) * 128].astype(F32), (128, 128)).T
            for j in range(PLANES):
                lanes = lax.broadcasted_iota(jnp.int32, (128, 128), 1) + j * 128
                kron_t[i * 128 : (i + 1) * 128, j * 128 : (j + 1) * 128] = jnp.where(
                    lanes.astype(F32) == column, 1.0, 0.0
                ).astype(BF16)

    def wait_hid():
        for copy in load_hid:
            copy.wait()

    def prepare():
        for copy in load_meta:
            copy.wait()
        earlier[...] = (
            lax.broadcasted_iota(jnp.int32, (TOKENS, TOKENS), 0)
            < lax.broadcasted_iota(jnp.int32, (TOKENS, TOKENS), 1)
        ).astype(F32).astype(BF16)

    def meta_arrivals():
        all_arrived(metas.at[0:7], sem_meta.at[1, 0])
        all_arrived(gate_rows.at[0:7], sem_meta.at[1, 1])

    def own_wait(k):
        own_tok[k].wait()

    def hid_pass():
        hid_wait(0)
        hid_send(4)
        hid_wait(1)
        hid_send(5)

    def hid_near():
        hid_wait(2)
        hid_wait(3)

    def hid_far():
        hid_wait(4)
        hid_wait(5)

    others(send_meta)
    ring_begin(0)
    ring_begin(1)
    wait_hid()
    transpose_half(0)
    hid_send(0)
    hid_send(3)
    transpose_half(1)
    hid_send(1)
    hid_send(2)
    late_loads()
    prepare()
    meta_arrivals()
    build(0)
    own_wait(0)
    pick(0, 0)
    build(1, -1)
    ring_forward(0, 1)
    pick(0, 1, -1)
    send_rows(0, 0)
    build(2, -2)
    own_wait(1)
    pick(1, 0)
    ring_forward(1, 1)
    pick(1, 1, -1)
    send_rows(1, 0)
    ring_forward(0, 2)
    pick(0, 2, -2)
    send_rows(0, 1)
    build(3, -3)
    ring_forward(1, 2)
    pick(1, 2, -2)
    send_rows(1, 1)
    build(4)
    build_kron()
    ring_forward(0, 3)
    ring_begin(2)
    pick(0, 3, -3)
    ring_forward(1, 3)
    ring_begin(3)
    pick(1, 3, -3)
    hid_pass()
    ring_forward(0, 4)
    pick(0, 4)
    send_rows(0, 2)
    ring_forward(2, 1)
    own_wait(2)
    pick(2, 0, 1, -1)
    ring_forward(1, 4)
    pick(1, 4)
    ring_forward(3, 1)
    hid_near()
    matmul_near()
    send_rows(1, 2)
    ring_forward(2, 2)
    pick(2, 2, -2)
    ring_forward(3, 2)
    hid_far()
    matmul_far()
    own_wait(3)
    pick(3, 0, 1, -1)
    ring_forward(2, 3)
    stage_matmul(1)
    send_rows(2, 0)
    ring_forward(3, 3)
    stage_forward(0)
    pick(3, 2, -2)
    pick(2, 3, -3)
    send_rows(2, 1)
    send_rows(3, 0)
    pick(3, 3, -3)
    send_rows(3, 1)
    ring_forward(2, 4)
    pick(2, 4)
    send_rows(2, 2)
    ring_forward(3, 4)
    pick(3, 4)
    send_rows(3, 2)
    stage_forward(1)
    latent_begin()
    stage_adam(0)
    stage_matmul(2)
    stage_matmul(3)
    stage_forward(2)
    stage_forward(3)
    stage_adam(1)
    stage_return(0)
    latent_end()
    stage_adam(2)
    drain_start()
    stage_return(1)
    stage_adam(3)
    drain_parts()
    stage_return(2)
    drain_out(0)
    drain_out(1)
    step_sent(2)
    stage_return(3)
    step_sent(3)
    drain_out(2)
    drain_out(3)


def expert_steps(*operands):
    anywhere = pl.BlockSpec(memory_space=pl.ANY)
    relays = [
        jax.ShapeDtypeStruct((2, PEERS, PLANES, ROWS, dc), BF16) for _, dc in CHUNKS
    ]
    returns = [
        jax.ShapeDtypeStruct((2, PLANES, PEERS, ROWS, dc), BF16) for _, dc in CHUNKS[: N - 1]
    ]
    shape = jax.ShapeDtypeStruct((2, PLANES, PEERS, ROWS, WIDTH), BF16)
    widest = max(dc for _, dc in CHUNKS)
    dma = pltpu.SemaphoreType.DMA
    scratch = [pltpu.VMEM((PLANES, TOKENS, dc), BF16) for _, dc in CHUNKS]
    scratch += [pltpu.VMEM((2, PEERS, PLANES, POS, dc), BF16) for _, dc in CHUNKS]
    scratch += [pltpu.VMEM((2, PLANES, PEERS, ROWS, dc), BF16) for _, dc in CHUNKS]
    scratch += [pltpu.VMEM((PEERS, 2, PLANES, POS, dc), BF16) for _, dc in CHUNKS]
    scratch += [pltpu.VMEM((2, PLANES, PEERS, ROWS, dc), BF16) for _, dc in CHUNKS[N - 1 :]]
    scratch += [
        pltpu.VMEM((PLANES, 4, TOKENS), jnp.int32),
        pltpu.VMEM((PLANES, 4, TOKENS), F32),
        pltpu.VMEM((PLANES, 16 * POS, TOKENS), BF16),
        pltpu.VMEM((2, 16 * POS, NEED), BF16),
        pltpu.VMEM((PLANES, 16 * POS, 128), F32),
        pltpu.VMEM((2, 4, PEERS, FPART, PLANES * POS), BF16),
        pltpu.VMEM((2, PEERS, 2, PLANES, ROWS, widest), BF16),
        pltpu.VMEM((2, 2, PLANES, PEERS, ROWS, widest), BF16),
        pltpu.VMEM((2, 2, PLANES * PEERS * ROWS, widest), BF16),
        pltpu.VMEM((1024, 1024), BF16),
        pltpu.VMEM((1024, 1024), BF16),
        pltpu.VMEM((TOKENS, TOKENS), BF16),
        pltpu.VMEM((PLANES * PEERS, CAP, 2, FPART), BF16),
        pltpu.VMEM((TOKENS, 1024), BF16),
        pltpu.VMEM((512, 1024), BF16),
        pltpu.VMEM((4, 128, TOKENS), F32),
        pltpu.VMEM((3, 128, TOKENS), F32),
        dma((2, 2)),
        dma((N, 2, 4, 2)),
        dma((2, N)),
        dma((7,)),
        dma((2, N)),
        dma((2, N)),
        dma((2, N)),
        dma((2, N)),
        dma((2, 8)),
        dma((2, N)),
        dma((2,)),
        dma((N + 9,)),
        dma((5, N)),
    ]
    results = pl.pallas_call(
        kernel,
        out_shape=[shape, jax.ShapeDtypeStruct((128, TOKENS), BF16)] + relays + returns,
        in_specs=[anywhere] * 4 + [pl.BlockSpec(memory_space=pltpu.VMEM)] + [anywhere] * 4,
        out_specs=[anywhere] * (2 * N + 1),
        scratch_shapes=scratch,
        compiler_params=pltpu.CompilerParams(
            collective_id=0, has_side_effects=True, vmem_limit_bytes=62 * 1024 * 1024
        ),
        cost_estimate=pl.CostEstimate(
            flops=50_000_000_000, bytes_accessed=60_000_000, transcendentals=2_000_000
        ),
    )(*operands)
    return results[0], results[1]


def hand_over_kernel(steps, latent, steps_out, latent_out, steps_held, latent_held, sem):
    pieces = [
        (steps.at[w, i], steps_held.at[w, i], steps_out.at[w, i])
        for w in range(2)
        for i in range(PLANES)
    ]
    pieces.append((latent, latent_held, latent_out))
    into = [
        pltpu.make_async_copy(a, b, sem.at[0, n]) for n, (a, b, _) in enumerate(pieces)
    ]
    back = [
        pltpu.make_async_copy(b, c, sem.at[1, n]) for n, (_, b, c) in enumerate(pieces)
    ]
    for copy in into:
        copy.start()
    for first, second in zip(into, back):
        first.wait()
        second.start()
    for copy in back:
        copy.wait()


def hand_over(*results):
    anywhere = pl.BlockSpec(memory_space=pl.ANY)
    return pl.pallas_call(
        hand_over_kernel,
        out_shape=[jax.ShapeDtypeStruct(r.shape, r.dtype) for r in results],
        in_specs=[anywhere] * 2,
        out_specs=[anywhere] * 2,
        scratch_shapes=[pltpu.VMEM(r.shape, r.dtype) for r in results]
        + [pltpu.SemaphoreType.DMA((2, 2 * PLANES + 1))],
    )(*results)


def shards(out_grad, routes, gates, dup_owner, hidden, moment1, moment2, value_grad, value_proj):
    experts = PLANES * PEERS
    hid = hidden[0].transpose(0, 2, 1, 3)
    steps, latent_grad = expert_steps(
        out_grad,
        routes.T,
        gates.T,
        hid,
        dup_owner.reshape(1, -1),
        moment1.reshape(experts * ROWS, WIDTH),
        moment2.reshape(experts * ROWS, WIDTH),
        value_grad,
        value_proj,
    )
    steps, latent_grad = hand_over(steps, latent_grad)
    return (steps.reshape(1, 2, PLANES * PEERS * ROWS, WIDTH), latent_grad)


def solution(mesh):
    in_specs = (
        P("expert", "dp"),
        P("expert", None),
        P("expert", None),
        P(),
        P("expert", None, None, None, "dp"),
        P(None, "expert", "dp"),
        P(None, "expert", "dp"),
        P("expert", "dp"),
        P(None, "dp"),
    )
    out_specs = (P("expert", None, None, "dp"), P("dp", "expert"))
    return jax.shard_map(shards, mesh=mesh, in_specs=in_specs, out_specs=out_specs, check_vma=False)
```

```python
import functools

import jax
import jax.numpy as jnp
from jax import lax
from jax.experimental import pallas as pl
from jax.experimental.pallas import tpu as pltpu
from jax.sharding import PartitionSpec as P

beta_first = 0.9
beta_second = 0.95
adam_eps = 1e-08
bias_first = 1.0 - 0.9**50 * 0.9**50
bias_second = 1.0 - 0.95**50 * 0.95**50

PLANES = 8
PEERS = 8
ROWS = 16
CAP = 30
POS = 32
TOKENS = 640
FPART = 256
WIDTH = 896
CHUNKS = ((0, 256), (256, 256), (512, 256), (768, 128))
N = len(CHUNKS)
ORDER = (0, 1, -1, 2, -2, 3, -3, 4)
GROUPS = ((0, 3), (3, 5), (5, 8))
HALF = TOKENS // 2
NEED = 16 * CAP
TURNS = (1, 7, 2, 6, 3, 5, 4)
MESH = pl.DeviceIdType.MESH
F32 = jnp.float32
BF16 = jnp.bfloat16


def kernel(
    og,
    routes,
    gates,
    hid,
    dup,
    m1,
    m2,
    vgrad,
    vproj,
    out,
    latent,
    *refs,
):
    relay_x, relay_s, refs = refs[:N], list(refs[N : 2 * N - 1]), refs[2 * N - 1 :]
    tok, refs = refs[:N], refs[N:]
    rows_in, refs = refs[:N], refs[N:]
    grad_in, refs = refs[:N], refs[N:]
    rows_out, refs = refs[:N], refs[N:]
    relay_s, refs = relay_s + list(refs[:1]), refs[1:]
    (
        metas,
        gate_rows,
        onehot,
        onehot_kept,
        gate_col,
        hid_t,
        part_out,
        step_out,
        mom,
        kron,
        kron_t,
        earlier,
        hid_raw,
        vg,
        vp,
        lat_part,
        lat_in,
        sem_meta,
        sem_ring,
        sem_ring_sent,
        sem_hid,
        sem_rows,
        sem_px,
        sem_pz,
        sem_sz,
        sem_last,
        sem_sx,
        sem_lat,
        sem_local,
        sem_own,
    ) = refs
    me = lax.axis_index("expert")
    y = lax.axis_index("dp")
    z = me // PEERS
    p = me % PEERS

    def plane(d):
        return lax.rem(z + d + PLANES, PLANES)

    def peer(d):
        return lax.rem(p + d + PEERS, PEERS)

    def dev_z(to):
        return {"expert": to * PEERS + p}

    def dev_p(to):
        return {"expert": z * PEERS + to}

    def dev_y(d):
        return {"dp": lax.rem(y + d + 4, 4)}

    def remote(src, dst, sent, arrived, device):
        return pltpu.make_async_remote_copy(
            src_ref=src,
            dst_ref=dst,
            send_sem=sent,
            recv_sem=arrived,
            device_id=device,
            device_id_type=MESH,
        )

    def all_sent(view, sem):
        remote(view, view, sem, sem, dev_p(p)).wait_send()

    def all_arrived(view, sem):
        remote(view, view, sem, sem, dev_p(p)).wait_recv()

    def others(body):
        def step(i, carry):
            body(i)
            return carry

        lax.fori_loop(1, 8, step, 0)

    def planes_in_turn(body):
        for i in TURNS:
            body(i)

    barrier = pltpu.get_barrier_semaphore()

    def greet(i):
        pl.semaphore_signal(barrier, inc=1, device_id=dev_z(plane(i)), device_id_type=MESH)
        pl.semaphore_signal(barrier, inc=1, device_id=dev_p(peer(i)), device_id_type=MESH)

    others(greet)
    for d in (1, 2, 3):
        pl.semaphore_signal(barrier, inc=1, device_id=dev_y(d), device_id_type=MESH)

    def local(src, dst, index):
        return pltpu.make_async_copy(src, dst, sem_local.at[index])

    own_tok = [
        local(og.at[:, pl.ds(CHUNKS[k][0], CHUNKS[k][1])], tok[k].at[z], k) for k in range(N)
    ]
    load_hid = [local(hid, hid_raw, N + 6)]
    load_latent = [local(vgrad, vg, N), local(vproj, vp, N + 7)]
    load_meta = [local(routes, metas.at[z], N + 1), local(gates, gate_rows.at[z], N + 8)]

    def load_moments(k):
        c0, dc = CHUNKS[k]
        return [
            local(
                m.at[:, pl.ds(c0, dc)],
                mom.at[k % 2, i, :, pl.ds(0, dc)],
                N + 2 + 2 * (k % 2) + i,
            )
            for i, m in enumerate((m1, m2))
        ]

    for copy in load_hid + load_meta + own_tok[:1]:
        copy.start()

    pl.semaphore_wait(barrier, 17)

    def meta_copies(i):
        return [
            remote(source, into.at[z], sem_meta.at[0, j], sem_meta.at[1, j], dev_z(plane(i)))
            for j, (source, into) in enumerate(((routes, metas), (gates, gate_rows)))
        ]

    def send_meta(i):
        for copy in meta_copies(i):
            copy.start()

    def late_loads():
        for copy in own_tok[1:] + load_latent:
            copy.start()
        for k in (0, 1):
            for copy in load_moments(k):
                copy.start()

    def last_step(k, way):
        return 4 if way == k % 2 else 3

    def ring_rows(k, way, step, half):
        size = HALF if step < last_step(k, way) else NEED // 2
        return pl.ds(half * size, size)

    def ring_sent(k, way, step):
        return sem_ring_sent.at[0 if step < last_step(k, way) else 1, k]

    def ring_send(k, way, step, half):
        c0, dc = CHUNKS[k]
        sign = 1 - 2 * way
        block = plane(-sign * (step - 1))
        rows = ring_rows(k, way, step, half)
        source = og.at[rows, pl.ds(c0, dc)] if step == 1 else tok[k].at[block, rows]
        arrived = sem_ring.at[k, way, step - 1, half]
        return remote(
            source, tok[k].at[block, rows], ring_sent(k, way, step), arrived, dev_z(plane(sign))
        )

    def ring_arrival(k, way, step, half):
        sign = 1 - 2 * way
        view = tok[k].at[plane(-sign * step), ring_rows(k, way, step, half)]
        arrived = sem_ring.at[k, way, step - 1, half]
        return remote(view, view, ring_sent(k, way, step), arrived, dev_z(plane(sign)))

    def ring_begin(k):
        for half in (0, 1):
            for way in (0, 1):
                ring_send(k, way, 1, half).start()

    def ring_forward(k, step):
        ways = [way for way in (0, 1) if step <= last_step(k, way)]
        for half in (0, 1):
            for way in ways:
                ring_arrival(k, way, step, half).wait_recv()
                if step + 1 < last_step(k, way):
                    ring_send(k, way, step + 1, half).start()
        for way in ways:
            if step + 1 == last_step(k, way):
                sign = 1 - 2 * way
                gather(k, -sign * step)
                block = plane(-sign * step)
                chosen = selection(needed(block, plane(sign)))
                kept = jnp.dot(chosen, tok[k][block], preferred_element_type=F32)
                tok[k][block, 0:NEED] = kept.astype(BF16)
                for half in (0, 1):
                    ring_send(k, way, step + 1, half).start()

    def needed(group, of_plane):
        match = jnp.where(lax.shift_right_logical(metas[group], 4) == of_plane, 1.0, 0.0)
        return jnp.max(match, axis=0, keepdims=True)

    def selection(need):
        before = jnp.dot(
            jnp.broadcast_to(need, (16, TOKENS)).astype(BF16),
            earlier[...],
            preferred_element_type=F32,
        )
        place = jnp.where(need > 0.5, before[0:1, :], -1.0)
        position = lax.broadcasted_iota(jnp.int32, (NEED, TOKENS), 0).astype(F32)
        return jnp.where(position == place, 1.0, 0.0).astype(BF16)

    def transpose_half(w):
        def piece(q, carry):
            empty = jnp.zeros((POS - CAP, FPART), BF16)
            for i, d in enumerate(ORDER):
                rows_out[1][q, w, i, 0:CAP] = hid_raw[plane(d) * PEERS + q, :, w, :]
                rows_out[1][q, w, i, CAP:POS] = empty
            hid_t[w, y, q] = rows_out[1][q, w].reshape(PLANES * POS, FPART).T
            return carry

        lax.fori_loop(0, PEERS, piece, 0)

    def y_part(d):
        return lax.rem(y + d + 4, 4)

    def hid_copy(index, w, part, d):
        view = hid_t.at[w, y_part(part)]
        return remote(view, view, sem_hid.at[6], sem_hid.at[index], dev_y(d))

    hid_copies = (
        (0, 0, 0, 1),
        (1, 1, 0, -1),
        (2, 1, 0, 1),
        (3, 0, 0, -1),
        (4, 0, -1, 1),
        (5, 1, 1, -1),
    )

    def hid_send(index):
        hid_copy(*hid_copies[index]).start()

    def hid_wait(index):
        number, w, part, d = hid_copies[index]
        hid_copy(number, w, part - d, d).wait_recv()

    def build_plane(d):
        i = plane(d)
        slot_of = lax.broadcasted_iota(jnp.int32, (16, TOKENS), 0) + z * 16
        named = jnp.zeros((16, TOKENS), F32)
        gate = jnp.zeros((16, TOKENS), F32)
        for k in range(4):
            match = slot_of == metas[i, k : k + 1, :]
            named = jnp.where(match, 1.0, named)
            gate = jnp.where(match, gate_rows[i, k : k + 1, :], gate)
        rank = jnp.dot(named.astype(BF16), earlier[...], preferred_element_type=F32)
        rank = jnp.where(named > 0.5, rank, -1.0)
        position = lax.broadcasted_iota(jnp.int32, (POS, TOKENS), 0).astype(F32)
        for s in range(16):
            chosen = position == rank[s : s + 1, :]
            onehot[i, s * POS : (s + 1) * POS, :] = jnp.where(chosen, 1.0, 0.0).astype(BF16)
            weight = jnp.sum(
                jnp.where(chosen, gate[s : s + 1, :], 0.0), axis=1, keepdims=True
            )
            gate_col[i, s * POS : (s + 1) * POS, :] = jnp.broadcast_to(weight, (POS, 128))
        if abs(d) >= 3:
            kept = lax.dot_general(
                (rank + 1.0).astype(BF16),
                selection(needed(i, z)),
                (((1,), (1,)), ((), ())),
                preferred_element_type=F32,
            )
            kept = kept - 1.0
            position = lax.broadcasted_iota(jnp.int32, (POS, NEED), 0).astype(F32)
            for s in range(16):
                chosen = jnp.where(position == kept[s : s + 1, :], 1.0, 0.0).astype(BF16)
                if d == 4:
                    onehot[i, s * POS : (s + 1) * POS, 0:NEED] = chosen
                else:
                    onehot_kept[(d + 3) // 6, s * POS : (s + 1) * POS, :] = chosen

    def build(*distances):
        for d in distances:
            build_plane(d)

    def gather(k, d):
        dc = CHUNKS[k][1]
        source, place = plane(d), ORDER.index(d)
        if d == 4:
            picks, rows = onehot[source, :, 0:NEED], tok[k][source, 0:NEED]
        elif d == (3 if k % 2 == 0 else -3):
            picks, rows = onehot_kept[(d + 3) // 6], tok[k][source, 0:NEED]
        else:
            picks, rows = onehot[source], tok[k][source]
        picked = jnp.dot(picks, rows, preferred_element_type=F32)
        for part in range(dc // 128):
            lanes = slice(part * 128, (part + 1) * 128)
            scaled = (picked[:, lanes] * gate_col[source]).astype(BF16)
            rows_out[k][:, :, place, :, lanes] = scaled.reshape(PEERS, 2, POS, 128)

    def rows_copy(k, group, to):
        low, high = GROUPS[group]
        return remote(
            rows_out[k].at[to, :, low:high],
            rows_in[k].at[:, p, low:high],
            sem_rows.at[0, k],
            sem_rows.at[1, k],
            dev_p(to),
        )

    def own(src, dst, stage, k):
        return pltpu.make_async_copy(src, dst, sem_own.at[stage, k])

    def rows_own(k):
        return own(rows_out[k].at[p], rows_in[k].at[:, p], 0, k)

    def pick(k, *distances):
        ahead = (-3, 2) if k % 2 == 0 else (3, -2)
        for d in distances:
            if d not in ahead:
                gather(k, d)

    def send_rows(k, group):
        others(lambda i: rows_copy(k, group, peer(i)).start())
        if group == len(GROUPS) - 1:
            rows_own(k).start()

    def lat_copy(d):
        return remote(
            lat_part.at[y_part(d)], lat_in.at[d - 1], sem_lat.at[0], sem_lat.at[1], dev_y(d)
        )

    def latent_begin():
        for copy in load_latent:
            copy.wait()
        for i in range(4):
            lat_part[i] = lax.dot_general(
                vp[i * 128 : (i + 1) * 128, :],
                vg[...],
                (((1,), (1,)), ((), ())),
                preferred_element_type=F32,
            )
        for d in (1, 2, 3):
            lat_copy(d).start()

    def latent_end():
        all_arrived(lat_in, sem_lat.at[1])
        total = lat_part[y] + lat_in[0] + lat_in[1] + lat_in[2]
        vp[0:128, 0:TOKENS] = total.astype(BF16)
        store = local(vp.at[pl.ds(0, 128), pl.ds(0, TOKENS)], latent, N + 7)
        store.start()
        store.wait()

    def part_view(k, to):
        return part_out.at[k % 2, to, :, :, :, pl.ds(0, CHUNKS[k][1])]

    def part_copy(k, to):
        return remote(
            part_view(k, to), relay_x[k].at[:, p], sem_px.at[0, k], sem_px.at[1, k], dev_p(to)
        )

    def part_sent(k):
        all_sent(part_out.at[k % 2, 0:7, :, :, :, pl.ds(0, CHUNKS[k][1])], sem_px.at[0, k])

    def part_own(k):
        return own(part_view(k, p), relay_x[k].at[:, p], 1, k)

    def stage_matmul(k):
        dc = CHUNKS[k][1]
        rows_own(k).wait()
        all_arrived(rows_in[k].at[:, 0:7], sem_rows.at[1, k])
        if k >= 2:
            part_sent(k - 2)

        matmul(k, 0, 1, 2, 3)
        part_own(k).start()
        others(lambda i: part_copy(k, peer(i)).start())

    def matmul(k, *offsets):
        dc = CHUNKS[k][1]

        def block(i, carry):
            w = lax.rem(i, 2)
            part = y_part(offsets[0] + i // 2)
            total = jnp.zeros((FPART, dc), F32)
            for q in range(PEERS):
                total += jnp.dot(
                    hid_t[w, part, q],
                    rows_in[k][w, q].reshape(PLANES * POS, dc),
                    preferred_element_type=F32,
                )
            rounded = total.astype(BF16).reshape(2, PEERS, ROWS, dc)
            for h in range(2):
                for q in range(PEERS):
                    part_out[k % 2, q, w, 2 * part + h, :, 0:dc] = rounded[h, q]
            return carry

        lax.fori_loop(0, 2 * len(offsets), block, 0)

    def piece_sends(d):
        planes = pl.ds(2 * y_part(d), 2)

        def send(i):
            to = peer(i)
            remote(
                part_out.at[0, to, :, planes, :, pl.ds(0, CHUNKS[0][1])],
                relay_x[0].at[:, p, planes],
                sem_px.at[0, 0],
                sem_px.at[1, 0],
                dev_p(to),
            ).start()

        others(send)

    def matmul_near():
        rows_own(0).wait()
        all_arrived(rows_in[0].at[:, 0:7], sem_rows.at[1, 0])
        for d in (0, 1, -1):
            matmul(0, d)
            piece_sends(d)

    def matmul_far():
        matmul(0, 2)
        piece_sends(2)
        part_own(0).start()

    def grad_copy(k, to):
        return remote(
            relay_x[k].at[:, :, to],
            grad_in[k].at[:, z],
            sem_pz.at[0, k],
            sem_pz.at[1, k],
            dev_z(to),
        )

    def grad_own(k):
        return own(relay_x[k].at[:, :, z], grad_in[k].at[:, z], 2, k)

    def stage_forward(k):
        part_own(k).wait()
        all_arrived(relay_x[k].at[:, 0:7], sem_px.at[1, k])
        planes_in_turn(lambda i: grad_copy(k, plane(i)).start())
        grad_own(k).start()

    def step_view(k, to):
        return step_out.at[k % 2, :, to, :, :, pl.ds(0, CHUNKS[k][1])]

    def step_copy(k, to, index):
        arrived = sem_sz.at[1, k] if k < N - 2 else sem_last.at[k - (N - 2), index]
        return remote(step_view(k, to), relay_s[k].at[:, z], sem_sz.at[0, k], arrived, dev_z(to))

    def step_sent(k):
        all_sent(step_out.at[k % 2, :, 0:7, :, :, pl.ds(0, CHUNKS[k][1])], sem_sz.at[0, k])

    def step_own(k):
        return own(step_view(k, z), relay_s[k].at[:, z], 3, k)

    tile = 256
    per_tile = tile // (PEERS * ROWS)

    def stage_adam(k):
        dc = CHUNKS[k][1]
        grad_own(k).wait()
        all_arrived(grad_in[k].at[:, 0:7], sem_pz.at[1, k])
        if k >= 2:
            step_sent(k - 2)
        for copy in load_moments(k):
            copy.wait()

        def block(i, carry):
            rows = pl.ds(pl.multiple_of(i * tile, tile), tile)
            planes = pl.ds(i * per_tile, per_tile)
            twins = grad_in[k][1].reshape(PLANES * PEERS * ROWS, dc)
            gradient = grad_in[k][0, planes].reshape(tile, dc).astype(F32)
            gradient += jnp.dot(kron[rows, :], twins, preferred_element_type=F32)
            first = beta_first * mom[k % 2, 0, rows, 0:dc].astype(F32)
            first += (1.0 - beta_first) * gradient
            second = beta_second * mom[k % 2, 1, rows, 0:dc].astype(F32)
            second += (1.0 - beta_second) * gradient * gradient
            value = first / bias_first / (jnp.sqrt(second / bias_second) + adam_eps)
            value = value.astype(BF16).reshape(per_tile, PEERS, ROWS, dc)
            step_out[k % 2, 0, planes, :, :, 0:dc] = value
            return carry

        lax.fori_loop(0, PLANES // per_tile, block, 0)

        def twin(i, carry):
            rows = pl.ds(pl.multiple_of(i * tile, tile), tile)
            planes = pl.ds(i * per_tile, per_tile)
            steps = step_out[k % 2, 0, :, :, :, 0:dc].reshape(PLANES * PEERS * ROWS, dc)
            value = jnp.dot(kron_t[rows, :], steps, preferred_element_type=F32)
            value = value.astype(BF16).reshape(per_tile, PEERS, ROWS, dc)
            step_out[k % 2, 1, planes, :, :, 0:dc] = value
            return carry

        lax.fori_loop(0, PLANES // per_tile, twin, 0)
        step_own(k).start()
        planes_in_turn(lambda i: step_copy(k, plane(i), i).start())
        if k + 2 < N:
            for copy in load_moments(k + 2):
                copy.start()

    def columns(k):
        return pl.ds(CHUNKS[k][0], CHUNKS[k][1])

    def out_copy(k, to):
        return remote(
            relay_s[k].at[:, :, to],
            out.at[:, :, p, :, columns(k)],
            sem_sx.at[0, k],
            sem_sx.at[1, k],
            dev_p(to),
        )

    def out_own(k):
        return own(relay_s[k].at[:, :, p], out.at[:, :, p, :, columns(k)], 4, k)

    def plane_copy(k, source, to):
        return remote(
            relay_s[k].at[:, source, to],
            out.at[:, source, p, :, columns(k)],
            sem_sx.at[0, k],
            sem_sx.at[1, k],
            dev_p(to),
        )

    def plane_own(k, source):
        return own(relay_s[k].at[:, source, p], out.at[:, source, p, :, columns(k)], 4, k)

    def stage_return(k):
        step_own(k).wait()
        if k < N - 2:
            all_arrived(relay_s[k].at[:, 0:7], sem_sz.at[1, k])
            out_own(k).start()
            others(lambda i: out_copy(k, peer(i)).start())
            return
        plane_own(k, z).start()
        others(lambda i: plane_copy(k, z, peer(i)).start())
        for index in TURNS:
            source = plane(-index)
            view = relay_s[k].at[:, source]
            remote(
                view, view, sem_sz.at[0, k], sem_last.at[k - (N - 2), index], dev_z(source)
            ).wait_recv()
            plane_own(k, source).start()
            others(lambda i: plane_copy(k, source, peer(i)).start())

    def drain_start():
        all_sent(metas.at[0:7], sem_meta.at[0, 0])
        all_sent(gate_rows.at[0:7], sem_meta.at[0, 1])
        all_sent(hid_t.at[:, 0:3], sem_hid.at[6])
        all_sent(lat_in, sem_lat.at[0])
        for k in range(N):
            all_sent(tok[k].at[0:5], sem_ring_sent.at[0, k])
            all_sent(tok[k].at[0:2, 0:NEED], sem_ring_sent.at[1, k])
            all_sent(rows_out[k].at[0:7], sem_rows.at[0, k])

    def drain_parts():
        for k in (N - 2, N - 1):
            part_sent(k)
        for k in range(N):
            all_sent(relay_x[k].at[:, :, 0:7], sem_pz.at[0, k])

    def drain_out(k):
        all_sent(relay_s[k].at[:, :, 0:7], sem_sx.at[0, k])
        all_arrived(out.at[:, :, 0:7, :, columns(k)], sem_sx.at[1, k])
        out_own(k).wait()

    def build_kron():
        spread = lax.broadcasted_iota(jnp.int32, (PLANES * PEERS, 1024), 1) // ROWS
        spread = spread == lax.broadcasted_iota(jnp.int32, (PLANES * PEERS, 1024), 0)
        owners = jnp.broadcast_to(dup[...].astype(F32), (16, PLANES * PEERS)).astype(BF16)
        owners = jnp.dot(owners, spread.astype(F32).astype(BF16), preferred_element_type=F32)
        offset = lax.broadcasted_iota(jnp.int32, (1, 1024), 1) % ROWS
        target = owners[0:1, :].astype(jnp.int32) * ROWS + offset
        for i in range(PLANES):
            rows = lax.broadcasted_iota(jnp.int32, (128, 1024), 0) + i * 128
            kron[i * 128 : (i + 1) * 128, :] = (
                jnp.where(rows == target, 1.0, 0.0).astype(BF16)
            )
            column = jnp.broadcast_to(target[:, i * 128 : (i + 1) * 128].astype(F32), (128, 128)).T
            for j in range(PLANES):
                lanes = lax.broadcasted_iota(jnp.int32, (128, 128), 1) + j * 128
                kron_t[i * 128 : (i + 1) * 128, j * 128 : (j + 1) * 128] = jnp.where(
                    lanes.astype(F32) == column, 1.0, 0.0
                ).astype(BF16)

    def wait_hid():
        for copy in load_hid:
            copy.wait()

    def prepare():
        for copy in load_meta:
            copy.wait()
        earlier[...] = (
            lax.broadcasted_iota(jnp.int32, (TOKENS, TOKENS), 0)
            < lax.broadcasted_iota(jnp.int32, (TOKENS, TOKENS), 1)
        ).astype(F32).astype(BF16)

    def meta_arrivals():
        all_arrived(metas.at[0:7], sem_meta.at[1, 0])
        all_arrived(gate_rows.at[0:7], sem_meta.at[1, 1])

    def own_wait(k):
        own_tok[k].wait()

    def hid_pass():
        hid_wait(0)
        hid_send(4)
        hid_wait(1)
        hid_send(5)

    def hid_near():
        hid_wait(2)
        hid_wait(3)

    def hid_far():
        hid_wait(4)
        hid_wait(5)

    others(send_meta)
    ring_begin(0)
    ring_begin(1)
    wait_hid()
    transpose_half(0)
    hid_send(0)
    hid_send(3)
    transpose_half(1)
    hid_send(1)
    hid_send(2)
    late_loads()
    prepare()
    meta_arrivals()
    build(0)
    own_wait(0)
    pick(0, 0)
    build(1, -1)
    ring_forward(0, 1)
    pick(0, 1, -1)
    send_rows(0, 0)
    build(2, -2)
    own_wait(1)
    pick(1, 0)
    ring_forward(1, 1)
    pick(1, 1, -1)
    send_rows(1, 0)
    ring_forward(0, 2)
    pick(0, 2, -2)
    send_rows(0, 1)
    build(3, -3)
    ring_forward(1, 2)
    pick(1, 2, -2)
    send_rows(1, 1)
    build(4)
    build_kron()
    ring_forward(0, 3)
    ring_begin(2)
    pick(0, 3, -3)
    ring_forward(1, 3)
    ring_begin(3)
    pick(1, 3, -3)
    hid_pass()
    ring_forward(0, 4)
    pick(0, 4)
    send_rows(0, 2)
    ring_forward(2, 1)
    own_wait(2)
    pick(2, 0, 1, -1)
    ring_forward(1, 4)
    pick(1, 4)
    ring_forward(3, 1)
    hid_near()
    matmul_near()
    ring_forward(2, 2)
    hid_far()
    matmul_far()
    send_rows(1, 2)
    pick(2, 2, -2)
    ring_forward(3, 2)
    own_wait(3)
    pick(3, 0, 1, -1)
    ring_forward(2, 3)
    stage_forward(0)
    ring_forward(3, 3)
    stage_matmul(1)
    send_rows(2, 0)
    pick(3, 2, -2)
    pick(2, 3, -3)
    send_rows(2, 1)
    send_rows(3, 0)
    pick(3, 3, -3)
    send_rows(3, 1)
    ring_forward(2, 4)
    pick(2, 4)
    send_rows(2, 2)
    stage_forward(1)
    ring_forward(3, 4)
    pick(3, 4)
    send_rows(3, 2)
    latent_begin()
    stage_adam(0)
    stage_matmul(2)
    stage_matmul(3)
    stage_forward(2)
    stage_forward(3)
    stage_adam(1)
    stage_return(0)
    latent_end()
    stage_adam(2)
    drain_start()
    stage_return(1)
    stage_adam(3)
    drain_parts()
    stage_return(2)
    drain_out(0)
    drain_out(1)
    step_sent(2)
    stage_return(3)
    step_sent(3)
    drain_out(2)
    drain_out(3)


def expert_steps(*operands):
    anywhere = pl.BlockSpec(memory_space=pl.ANY)
    relays = [
        jax.ShapeDtypeStruct((2, PEERS, PLANES, ROWS, dc), BF16) for _, dc in CHUNKS
    ]
    returns = [
        jax.ShapeDtypeStruct((2, PLANES, PEERS, ROWS, dc), BF16) for _, dc in CHUNKS[: N - 1]
    ]
    shape = jax.ShapeDtypeStruct((2, PLANES, PEERS, ROWS, WIDTH), BF16)
    widest = max(dc for _, dc in CHUNKS)
    dma = pltpu.SemaphoreType.DMA
    scratch = [pltpu.VMEM((PLANES, TOKENS, dc), BF16) for _, dc in CHUNKS]
    scratch += [pltpu.VMEM((2, PEERS, PLANES, POS, dc), BF16) for _, dc in CHUNKS]
    scratch += [pltpu.VMEM((2, PLANES, PEERS, ROWS, dc), BF16) for _, dc in CHUNKS]
    scratch += [pltpu.VMEM((PEERS, 2, PLANES, POS, dc), BF16) for _, dc in CHUNKS]
    scratch += [pltpu.VMEM((2, PLANES, PEERS, ROWS, dc), BF16) for _, dc in CHUNKS[N - 1 :]]
    scratch += [
        pltpu.VMEM((PLANES, 4, TOKENS), jnp.int32),
        pltpu.VMEM((PLANES, 4, TOKENS), F32),
        pltpu.VMEM((PLANES, 16 * POS, TOKENS), BF16),
        pltpu.VMEM((2, 16 * POS, NEED), BF16),
        pltpu.VMEM((PLANES, 16 * POS, 128), F32),
        pltpu.VMEM((2, 4, PEERS, FPART, PLANES * POS), BF16),
        pltpu.VMEM((2, PEERS, 2, PLANES, ROWS, widest), BF16),
        pltpu.VMEM((2, 2, PLANES, PEERS, ROWS, widest), BF16),
        pltpu.VMEM((2, 2, PLANES * PEERS * ROWS, widest), BF16),
        pltpu.VMEM((1024, 1024), BF16),
        pltpu.VMEM((1024, 1024), BF16),
        pltpu.VMEM((TOKENS, TOKENS), BF16),
        pltpu.VMEM((PLANES * PEERS, CAP, 2, FPART), BF16),
        pltpu.VMEM((TOKENS, 1024), BF16),
        pltpu.VMEM((512, 1024), BF16),
        pltpu.VMEM((4, 128, TOKENS), F32),
        pltpu.VMEM((3, 128, TOKENS), F32),
        dma((2, 2)),
        dma((N, 2, 4, 2)),
        dma((2, N)),
        dma((7,)),
        dma((2, N)),
        dma((2, N)),
        dma((2, N)),
        dma((2, N)),
        dma((2, 8)),
        dma((2, N)),
        dma((2,)),
        dma((N + 9,)),
        dma((5, N)),
    ]
    results = pl.pallas_call(
        kernel,
        out_shape=[shape, jax.ShapeDtypeStruct((128, TOKENS), BF16)] + relays + returns,
        in_specs=[anywhere] * 4 + [pl.BlockSpec(memory_space=pltpu.VMEM)] + [anywhere] * 4,
        out_specs=[anywhere] * (2 * N + 1),
        scratch_shapes=scratch,
        compiler_params=pltpu.CompilerParams(
            collective_id=0, has_side_effects=True, vmem_limit_bytes=62 * 1024 * 1024
        ),
        cost_estimate=pl.CostEstimate(
            flops=50_000_000_000, bytes_accessed=60_000_000, transcendentals=2_000_000
        ),
    )(*operands)
    return results[0], results[1]


def hand_over_kernel(steps, latent, steps_out, latent_out, steps_held, latent_held, sem):
    pieces = [
        (steps.at[w, i], steps_held.at[w, i], steps_out.at[w, i])
        for w in range(2)
        for i in range(PLANES)
    ]
    pieces.append((latent, latent_held, latent_out))
    into = [
        pltpu.make_async_copy(a, b, sem.at[0, n]) for n, (a, b, _) in enumerate(pieces)
    ]
    back = [
        pltpu.make_async_copy(b, c, sem.at[1, n]) for n, (_, b, c) in enumerate(pieces)
    ]
    for copy in into:
        copy.start()
    for first, second in zip(into, back):
        first.wait()
        second.start()
    for copy in back:
        copy.wait()


def hand_over(*results):
    anywhere = pl.BlockSpec(memory_space=pl.ANY)
    return pl.pallas_call(
        hand_over_kernel,
        out_shape=[jax.ShapeDtypeStruct(r.shape, r.dtype) for r in results],
        in_specs=[anywhere] * 2,
        out_specs=[anywhere] * 2,
        scratch_shapes=[pltpu.VMEM(r.shape, r.dtype) for r in results]
        + [pltpu.SemaphoreType.DMA((2, 2 * PLANES + 1))],
    )(*results)


def shards(out_grad, routes, gates, dup_owner, hidden, moment1, moment2, value_grad, value_proj):
    experts = PLANES * PEERS
    hid = hidden[0].transpose(0, 2, 1, 3)
    steps, latent_grad = expert_steps(
        out_grad,
        routes.T,
        gates.T,
        hid,
        dup_owner.reshape(1, -1),
        moment1.reshape(experts * ROWS, WIDTH),
        moment2.reshape(experts * ROWS, WIDTH),
        value_grad,
        value_proj,
    )
    steps, latent_grad = hand_over(steps, latent_grad)
    return (steps.reshape(1, 2, PLANES * PEERS * ROWS, WIDTH), latent_grad)


def solution(mesh):
    in_specs = (
        P("expert", "dp"),
        P("expert", None),
        P("expert", None),
        P(),
        P("expert", None, None, None, "dp"),
        P(None, "expert", "dp"),
        P(None, "expert", "dp"),
        P("expert", "dp"),
        P(None, "dp"),
    )
    out_specs = (P("expert", None, None, "dp"), P("dp", "expert"))
    return jax.shard_map(shards, mesh=mesh, in_specs=in_specs, out_specs=out_specs, check_vma=False)
```

```python
import functools

import jax
import jax.numpy as jnp
from jax import lax
from jax.experimental import pallas as pl
from jax.experimental.pallas import tpu as pltpu
from jax.sharding import PartitionSpec as P

beta_first = 0.9
beta_second = 0.95
adam_eps = 1e-08
bias_first = 1.0 - 0.9**50 * 0.9**50
bias_second = 1.0 - 0.95**50 * 0.95**50

PLANES = 8
PEERS = 8
ROWS = 16
CAP = 30
POS = 32
TOKENS = 640
FPART = 256
WIDTH = 896
CHUNKS = ((0, 256), (256, 256), (512, 256), (768, 128))
N = len(CHUNKS)
ORDER = (0, 1, -1, 2, -2, 3, -3, 4)
GROUPS = ((0, 3), (3, 5), (5, 8))
HALF = TOKENS // 2
NEED = 16 * CAP
TURNS = (1, 7, 2, 6, 3, 5, 4)
MESH = pl.DeviceIdType.MESH
F32 = jnp.float32
BF16 = jnp.bfloat16


def kernel(
    og,
    routes,
    gates,
    hid,
    dup,
    m1,
    m2,
    vgrad,
    vproj,
    out,
    latent,
    *refs,
):
    relay_x, relay_s, refs = refs[:N], list(refs[N : 2 * N - 1]), refs[2 * N - 1 :]
    tok, refs = refs[:N], refs[N:]
    rows_in, refs = refs[:N], refs[N:]
    grad_in, refs = refs[:N], refs[N:]
    rows_out, refs = refs[:N], refs[N:]
    relay_s, refs = relay_s + list(refs[:1]), refs[1:]
    (
        metas,
        gate_rows,
        onehot,
        onehot_kept,
        gate_col,
        hid_t,
        part_out,
        step_out,
        mom,
        kron,
        kron_t,
        earlier,
        hid_raw,
        vg,
        vp,
        lat_part,
        lat_in,
        sem_meta,
        sem_ring,
        sem_ring_sent,
        sem_hid,
        sem_rows,
        sem_px,
        sem_pz,
        sem_sz,
        sem_last,
        sem_sx,
        sem_lat,
        sem_local,
        sem_own,
    ) = refs
    me = lax.axis_index("expert")
    y = lax.axis_index("dp")
    z = me // PEERS
    p = me % PEERS

    def plane(d):
        return lax.rem(z + d + PLANES, PLANES)

    def peer(d):
        return lax.rem(p + d + PEERS, PEERS)

    def dev_z(to):
        return {"expert": to * PEERS + p}

    def dev_p(to):
        return {"expert": z * PEERS + to}

    def dev_y(d):
        return {"dp": lax.rem(y + d + 4, 4)}

    def remote(src, dst, sent, arrived, device):
        return pltpu.make_async_remote_copy(
            src_ref=src,
            dst_ref=dst,
            send_sem=sent,
            recv_sem=arrived,
            device_id=device,
            device_id_type=MESH,
        )

    def all_sent(view, sem):
        remote(view, view, sem, sem, dev_p(p)).wait_send()

    def all_arrived(view, sem):
        remote(view, view, sem, sem, dev_p(p)).wait_recv()

    def others(body):
        def step(i, carry):
            body(i)
            return carry

        lax.fori_loop(1, 8, step, 0)

    def planes_in_turn(body):
        for i in TURNS:
            body(i)

    barrier = pltpu.get_barrier_semaphore()

    def greet(i):
        pl.semaphore_signal(barrier, inc=1, device_id=dev_z(plane(i)), device_id_type=MESH)
        pl.semaphore_signal(barrier, inc=1, device_id=dev_p(peer(i)), device_id_type=MESH)

    others(greet)
    for d in (1, 2, 3):
        pl.semaphore_signal(barrier, inc=1, device_id=dev_y(d), device_id_type=MESH)

    def local(src, dst, index):
        return pltpu.make_async_copy(src, dst, sem_local.at[index])

    own_tok = [
        local(og.at[:, pl.ds(CHUNKS[k][0], CHUNKS[k][1])], tok[k].at[z], k) for k in range(N)
    ]
    load_hid = [local(hid, hid_raw, N + 6)]
    load_latent = [local(vgrad, vg, N), local(vproj, vp, N + 7)]
    load_meta = [local(routes, metas.at[z], N + 1), local(gates, gate_rows.at[z], N + 8)]

    def load_moments(k):
        c0, dc = CHUNKS[k]
        return [
            local(
                m.at[:, pl.ds(c0, dc)],
                mom.at[k % 2, i, :, pl.ds(0, dc)],
                N + 2 + 2 * (k % 2) + i,
            )
            for i, m in enumerate((m1, m2))
        ]

    for copy in load_hid + load_meta + own_tok[:1]:
        copy.start()

    pl.semaphore_wait(barrier, 17)

    def meta_copies(i):
        return [
            remote(source, into.at[z], sem_meta.at[0, j], sem_meta.at[1, j], dev_z(plane(i)))
            for j, (source, into) in enumerate(((routes, metas), (gates, gate_rows)))
        ]

    def send_meta(i):
        for copy in meta_copies(i):
            copy.start()

    def late_loads():
        for copy in own_tok[1:] + load_latent:
            copy.start()
        for k in (0, 1):
            for copy in load_moments(k):
                copy.start()

    def last_step(k, way):
        return 4 if way == k % 2 else 3

    def ring_rows(k, way, step, half):
        size = HALF if step < last_step(k, way) else NEED // 2
        return pl.ds(half * size, size)

    def ring_sent(k, way, step):
        return sem_ring_sent.at[0 if step < last_step(k, way) else 1, k]

    def ring_send(k, way, step, half):
        c0, dc = CHUNKS[k]
        sign = 1 - 2 * way
        block = plane(-sign * (step - 1))
        rows = ring_rows(k, way, step, half)
        source = og.at[rows, pl.ds(c0, dc)] if step == 1 else tok[k].at[block, rows]
        arrived = sem_ring.at[k, way, step - 1, half]
        return remote(
            source, tok[k].at[block, rows], ring_sent(k, way, step), arrived, dev_z(plane(sign))
        )

    def ring_arrival(k, way, step, half):
        sign = 1 - 2 * way
        view = tok[k].at[plane(-sign * step), ring_rows(k, way, step, half)]
        arrived = sem_ring.at[k, way, step - 1, half]
        return remote(view, view, ring_sent(k, way, step), arrived, dev_z(plane(sign)))

    def ring_begin(k):
        for half in (0, 1):
            for way in (0, 1):
                ring_send(k, way, 1, half).start()

    def ring_forward(k, step):
        ways = [way for way in (0, 1) if step <= last_step(k, way)]
        for half in (0, 1):
            for way in ways:
                ring_arrival(k, way, step, half).wait_recv()
                if step + 1 < last_step(k, way):
                    ring_send(k, way, step + 1, half).start()
        for way in ways:
            if step + 1 == last_step(k, way):
                sign = 1 - 2 * way
                gather(k, -sign * step)
                block = plane(-sign * step)
                chosen = selection(needed(block, plane(sign)))
                kept = jnp.dot(chosen, tok[k][block], preferred_element_type=F32)
                tok[k][block, 0:NEED] = kept.astype(BF16)
                for half in (0, 1):
                    ring_send(k, way, step + 1, half).start()

    def needed(group, of_plane):
        match = jnp.where(lax.shift_right_logical(metas[group], 4) == of_plane, 1.0, 0.0)
        return jnp.max(match, axis=0, keepdims=True)

    def selection(need):
        before = jnp.dot(
            jnp.broadcast_to(need, (16, TOKENS)).astype(BF16),
            earlier[...],
            preferred_element_type=F32,
        )
        place = jnp.where(need > 0.5, before[0:1, :], -1.0)
        position = lax.broadcasted_iota(jnp.int32, (NEED, TOKENS), 0).astype(F32)
        return jnp.where(position == place, 1.0, 0.0).astype(BF16)

    def transpose_half(w):
        def piece(q, carry):
            empty = jnp.zeros((POS - CAP, FPART), BF16)
            for i, d in enumerate(ORDER):
                rows_out[1][q, w, i, 0:CAP] = hid_raw[plane(d) * PEERS + q, :, w, :]
                rows_out[1][q, w, i, CAP:POS] = empty
            hid_t[w, y, q] = rows_out[1][q, w].reshape(PLANES * POS, FPART).T
            return carry

        lax.fori_loop(0, PEERS, piece, 0)

    def y_part(d):
        return lax.rem(y + d + 4, 4)

    def hid_copy(index, w, part, d):
        view = hid_t.at[w, y_part(part)]
        return remote(view, view, sem_hid.at[6], sem_hid.at[index], dev_y(d))

    hid_copies = (
        (0, 0, 0, 1),
        (1, 1, 0, -1),
        (2, 1, 0, 1),
        (3, 0, 0, -1),
        (4, 0, -1, 1),
        (5, 1, 1, -1),
    )

    def hid_send(index):
        hid_copy(*hid_copies[index]).start()

    def hid_wait(index):
        number, w, part, d = hid_copies[index]
        hid_copy(number, w, part - d, d).wait_recv()

    def build_plane(d):
        i = plane(d)
        slot_of = lax.broadcasted_iota(jnp.int32, (16, TOKENS), 0) + z * 16
        named = jnp.zeros((16, TOKENS), F32)
        gate = jnp.zeros((16, TOKENS), F32)
        for k in range(4):
            match = slot_of == metas[i, k : k + 1, :]
            named = jnp.where(match, 1.0, named)
            gate = jnp.where(match, gate_rows[i, k : k + 1, :], gate)
        rank = jnp.dot(named.astype(BF16), earlier[...], preferred_element_type=F32)
        rank = jnp.where(named > 0.5, rank, -1.0)
        position = lax.broadcasted_iota(jnp.int32, (POS, TOKENS), 0).astype(F32)
        for s in range(16):
            chosen = position == rank[s : s + 1, :]
            onehot[i, s * POS : (s + 1) * POS, :] = jnp.where(chosen, 1.0, 0.0).astype(BF16)
            weight = jnp.sum(
                jnp.where(chosen, gate[s : s + 1, :], 0.0), axis=1, keepdims=True
            )
            gate_col[i, s * POS : (s + 1) * POS, :] = jnp.broadcast_to(weight, (POS, 128))
        if abs(d) >= 3:
            kept = lax.dot_general(
                (rank + 1.0).astype(BF16),
                selection(needed(i, z)),
                (((1,), (1,)), ((), ())),
                preferred_element_type=F32,
            )
            kept = kept - 1.0
            position = lax.broadcasted_iota(jnp.int32, (POS, NEED), 0).astype(F32)
            for s in range(16):
                chosen = jnp.where(position == kept[s : s + 1, :], 1.0, 0.0).astype(BF16)
                if d == 4:
                    onehot[i, s * POS : (s + 1) * POS, 0:NEED] = chosen
                else:
                    onehot_kept[(d + 3) // 6, s * POS : (s + 1) * POS, :] = chosen

    def build(*distances):
        for d in distances:
            build_plane(d)

    def gather(k, d):
        dc = CHUNKS[k][1]
        source, place = plane(d), ORDER.index(d)
        if d == 4:
            picks, rows = onehot[source, :, 0:NEED], tok[k][source, 0:NEED]
        elif d == (3 if k % 2 == 0 else -3):
            picks, rows = onehot_kept[(d + 3) // 6], tok[k][source, 0:NEED]
        else:
            picks, rows = onehot[source], tok[k][source]
        picked = jnp.dot(picks, rows, preferred_element_type=F32)
        for part in range(dc // 128):
            lanes = slice(part * 128, (part + 1) * 128)
            scaled = (picked[:, lanes] * gate_col[source]).astype(BF16)
            rows_out[k][:, :, place, :, lanes] = scaled.reshape(PEERS, 2, POS, 128)

    def rows_copy(k, group, to):
        low, high = GROUPS[group]
        return remote(
            rows_out[k].at[to, :, low:high],
            rows_in[k].at[:, p, low:high],
            sem_rows.at[0, k],
            sem_rows.at[1, k],
            dev_p(to),
        )

    def own(src, dst, stage, k):
        return pltpu.make_async_copy(src, dst, sem_own.at[stage, k])

    def rows_own(k):
        return own(rows_out[k].at[p], rows_in[k].at[:, p], 0, k)

    def pick(k, *distances):
        ahead = (-3, 2) if k % 2 == 0 else (3, -2)
        for d in distances:
            if d not in ahead:
                gather(k, d)

    def send_rows(k, group):
        others(lambda i: rows_copy(k, group, peer(i)).start())
        if group == len(GROUPS) - 1:
            rows_own(k).start()

    def lat_copy(d):
        return remote(
            lat_part.at[y_part(d)], lat_in.at[d - 1], sem_lat.at[0], sem_lat.at[1], dev_y(d)
        )

    def latent_begin():
        for copy in load_latent:
            copy.wait()
        for i in range(4):
            lat_part[i] = lax.dot_general(
                vp[i * 128 : (i + 1) * 128, :],
                vg[...],
                (((1,), (1,)), ((), ())),
                preferred_element_type=F32,
            )
        for d in (1, 2, 3):
            lat_copy(d).start()

    def latent_end():
        all_arrived(lat_in, sem_lat.at[1])
        total = lat_part[y] + lat_in[0] + lat_in[1] + lat_in[2]
        vp[0:128, 0:TOKENS] = total.astype(BF16)
        store = local(vp.at[pl.ds(0, 128), pl.ds(0, TOKENS)], latent, N + 7)
        store.start()
        store.wait()

    def part_view(k, to):
        return part_out.at[k % 2, to, :, :, :, pl.ds(0, CHUNKS[k][1])]

    def part_copy(k, to):
        return remote(
            part_view(k, to), relay_x[k].at[:, p], sem_px.at[0, k], sem_px.at[1, k], dev_p(to)
        )

    def part_sent(k):
        all_sent(part_out.at[k % 2, 0:7, :, :, :, pl.ds(0, CHUNKS[k][1])], sem_px.at[0, k])

    def part_own(k):
        return own(part_view(k, p), relay_x[k].at[:, p], 1, k)

    def stage_matmul(k):
        dc = CHUNKS[k][1]
        rows_own(k).wait()
        all_arrived(rows_in[k].at[:, 0:7], sem_rows.at[1, k])
        if k >= 2:
            part_sent(k - 2)

        matmul(k, 0, 1, 2, 3)
        part_own(k).start()
        others(lambda i: part_copy(k, peer(i)).start())

    def matmul(k, *offsets):
        dc = CHUNKS[k][1]

        def block(i, carry):
            w = lax.rem(i, 2)
            part = y_part(offsets[0] + i // 2)
            total = jnp.zeros((FPART, dc), F32)
            for q in range(PEERS):
                total += jnp.dot(
                    hid_t[w, part, q],
                    rows_in[k][w, q].reshape(PLANES * POS, dc),
                    preferred_element_type=F32,
                )
            rounded = total.astype(BF16).reshape(2, PEERS, ROWS, dc)
            for h in range(2):
                for q in range(PEERS):
                    part_out[k % 2, q, w, 2 * part + h, :, 0:dc] = rounded[h, q]
            return carry

        lax.fori_loop(0, 2 * len(offsets), block, 0)

    def piece_sends(d):
        planes = pl.ds(2 * y_part(d), 2)

        def send(i):
            to = peer(i)
            remote(
                part_out.at[0, to, :, planes, :, pl.ds(0, CHUNKS[0][1])],
                relay_x[0].at[:, p, planes],
                sem_px.at[0, 0],
                sem_px.at[1, 0],
                dev_p(to),
            ).start()

        others(send)

    def matmul_near():
        rows_own(0).wait()
        all_arrived(rows_in[0].at[:, 0:7], sem_rows.at[1, 0])
        for d in (0, 1, -1):
            matmul(0, d)
            piece_sends(d)

    def matmul_far():
        matmul(0, 2)
        piece_sends(2)
        part_own(0).start()

    def grad_copy(k, to):
        return remote(
            relay_x[k].at[:, :, to],
            grad_in[k].at[:, z],
            sem_pz.at[0, k],
            sem_pz.at[1, k],
            dev_z(to),
        )

    def grad_own(k):
        return own(relay_x[k].at[:, :, z], grad_in[k].at[:, z], 2, k)

    def stage_forward(k):
        part_own(k).wait()
        all_arrived(relay_x[k].at[:, 0:7], sem_px.at[1, k])
        planes_in_turn(lambda i: grad_copy(k, plane(i)).start())
        grad_own(k).start()

    def step_view(k, to):
        return step_out.at[k % 2, :, to, :, :, pl.ds(0, CHUNKS[k][1])]

    def step_copy(k, to, index):
        arrived = sem_sz.at[1, k] if k < N - 2 else sem_last.at[k - (N - 2), index]
        return remote(step_view(k, to), relay_s[k].at[:, z], sem_sz.at[0, k], arrived, dev_z(to))

    def step_sent(k):
        all_sent(step_out.at[k % 2, :, 0:7, :, :, pl.ds(0, CHUNKS[k][1])], sem_sz.at[0, k])

    def step_own(k):
        return own(step_view(k, z), relay_s[k].at[:, z], 3, k)

    tile = 256
    per_tile = tile // (PEERS * ROWS)

    def stage_adam(k):
        dc = CHUNKS[k][1]
        grad_own(k).wait()
        all_arrived(grad_in[k].at[:, 0:7], sem_pz.at[1, k])
        if k >= 2:
            step_sent(k - 2)
        for copy in load_moments(k):
            copy.wait()

        def block(i, carry):
            rows = pl.ds(pl.multiple_of(i * tile, tile), tile)
            planes = pl.ds(i * per_tile, per_tile)
            twins = grad_in[k][1].reshape(PLANES * PEERS * ROWS, dc)
            gradient = grad_in[k][0, planes].reshape(tile, dc).astype(F32)
            gradient += jnp.dot(kron[rows, :], twins, preferred_element_type=F32)
            first = beta_first * mom[k % 2, 0, rows, 0:dc].astype(F32)
            first += (1.0 - beta_first) * gradient
            second = beta_second * mom[k % 2, 1, rows, 0:dc].astype(F32)
            second += (1.0 - beta_second) * gradient * gradient
            value = first / bias_first / (jnp.sqrt(second / bias_second) + adam_eps)
            value = value.astype(BF16).reshape(per_tile, PEERS, ROWS, dc)
            step_out[k % 2, 0, planes, :, :, 0:dc] = value
            return carry

        lax.fori_loop(0, PLANES // per_tile, block, 0)

        def twin(i, carry):
            rows = pl.ds(pl.multiple_of(i * tile, tile), tile)
            planes = pl.ds(i * per_tile, per_tile)
            steps = step_out[k % 2, 0, :, :, :, 0:dc].reshape(PLANES * PEERS * ROWS, dc)
            value = jnp.dot(kron_t[rows, :], steps, preferred_element_type=F32)
            value = value.astype(BF16).reshape(per_tile, PEERS, ROWS, dc)
            step_out[k % 2, 1, planes, :, :, 0:dc] = value
            return carry

        lax.fori_loop(0, PLANES // per_tile, twin, 0)
        step_own(k).start()
        planes_in_turn(lambda i: step_copy(k, plane(i), i).start())
        if k + 2 < N:
            for copy in load_moments(k + 2):
                copy.start()

    def columns(k):
        return pl.ds(CHUNKS[k][0], CHUNKS[k][1])

    def out_copy(k, to):
        return remote(
            relay_s[k].at[:, :, to],
            out.at[:, :, p, :, columns(k)],
            sem_sx.at[0, k],
            sem_sx.at[1, k],
            dev_p(to),
        )

    def out_own(k):
        return own(relay_s[k].at[:, :, p], out.at[:, :, p, :, columns(k)], 4, k)

    def plane_copy(k, source, to):
        return remote(
            relay_s[k].at[:, source, to],
            out.at[:, source, p, :, columns(k)],
            sem_sx.at[0, k],
            sem_sx.at[1, k],
            dev_p(to),
        )

    def plane_own(k, source):
        return own(relay_s[k].at[:, source, p], out.at[:, source, p, :, columns(k)], 4, k)

    def stage_return(k):
        step_own(k).wait()
        if k < N - 2:
            all_arrived(relay_s[k].at[:, 0:7], sem_sz.at[1, k])
            out_own(k).start()
            others(lambda i: out_copy(k, peer(i)).start())
            return
        plane_own(k, z).start()
        others(lambda i: plane_copy(k, z, peer(i)).start())
        for index in TURNS:
            source = plane(-index)
            view = relay_s[k].at[:, source]
            remote(
                view, view, sem_sz.at[0, k], sem_last.at[k - (N - 2), index], dev_z(source)
            ).wait_recv()
            plane_own(k, source).start()
            others(lambda i: plane_copy(k, source, peer(i)).start())

    def drain_start():
        all_sent(metas.at[0:7], sem_meta.at[0, 0])
        all_sent(gate_rows.at[0:7], sem_meta.at[0, 1])
        all_sent(hid_t.at[:, 0:3], sem_hid.at[6])
        all_sent(lat_in, sem_lat.at[0])
        for k in range(N):
            all_sent(tok[k].at[0:5], sem_ring_sent.at[0, k])
            all_sent(tok[k].at[0:2, 0:NEED], sem_ring_sent.at[1, k])
            all_sent(rows_out[k].at[0:7], sem_rows.at[0, k])

    def drain_parts():
        for k in (N - 2, N - 1):
            part_sent(k)
        for k in range(N):
            all_sent(relay_x[k].at[:, :, 0:7], sem_pz.at[0, k])

    def drain_out(k):
        all_sent(relay_s[k].at[:, :, 0:7], sem_sx.at[0, k])
        all_arrived(out.at[:, :, 0:7, :, columns(k)], sem_sx.at[1, k])
        out_own(k).wait()

    def build_kron():
        spread = lax.broadcasted_iota(jnp.int32, (PLANES * PEERS, 1024), 1) // ROWS
        spread = spread == lax.broadcasted_iota(jnp.int32, (PLANES * PEERS, 1024), 0)
        owners = jnp.broadcast_to(dup[...].astype(F32), (16, PLANES * PEERS)).astype(BF16)
        owners = jnp.dot(owners, spread.astype(F32).astype(BF16), preferred_element_type=F32)
        offset = lax.broadcasted_iota(jnp.int32, (1, 1024), 1) % ROWS
        target = owners[0:1, :].astype(jnp.int32) * ROWS + offset
        for i in range(PLANES):
            rows = lax.broadcasted_iota(jnp.int32, (128, 1024), 0) + i * 128
            kron[i * 128 : (i + 1) * 128, :] = (
                jnp.where(rows == target, 1.0, 0.0).astype(BF16)
            )
            column = jnp.broadcast_to(target[:, i * 128 : (i + 1) * 128].astype(F32), (128, 128)).T
            for j in range(PLANES):
                lanes = lax.broadcasted_iota(jnp.int32, (128, 128), 1) + j * 128
                kron_t[i * 128 : (i + 1) * 128, j * 128 : (j + 1) * 128] = jnp.where(
                    lanes.astype(F32) == column, 1.0, 0.0
                ).astype(BF16)

    def wait_hid():
        for copy in load_hid:
            copy.wait()

    def prepare():
        for copy in load_meta:
            copy.wait()
        earlier[...] = (
            lax.broadcasted_iota(jnp.int32, (TOKENS, TOKENS), 0)
            < lax.broadcasted_iota(jnp.int32, (TOKENS, TOKENS), 1)
        ).astype(F32).astype(BF16)

    def meta_arrivals():
        all_arrived(metas.at[0:7], sem_meta.at[1, 0])
        all_arrived(gate_rows.at[0:7], sem_meta.at[1, 1])

    def own_wait(k):
        own_tok[k].wait()

    def hid_pass():
        hid_wait(0)
        hid_send(4)
        hid_wait(1)
        hid_send(5)

    def hid_near():
        hid_wait(2)
        hid_wait(3)

    def hid_far():
        hid_wait(4)
        hid_wait(5)

    others(send_meta)
    ring_begin(0)
    ring_begin(1)
    wait_hid()
    transpose_half(0)
    hid_send(0)
    hid_send(3)
    transpose_half(1)
    hid_send(1)
    hid_send(2)
    late_loads()
    prepare()
    meta_arrivals()
    build(0)
    own_wait(0)
    pick(0, 0)
    build(1, -1)
    ring_forward(0, 1)
    pick(0, 1, -1)
    send_rows(0, 0)
    build(2, -2)
    own_wait(1)
    pick(1, 0)
    ring_forward(1, 1)
    pick(1, 1, -1)
    send_rows(1, 0)
    ring_forward(0, 2)
    pick(0, 2, -2)
    send_rows(0, 1)
    build(3, -3)
    ring_forward(1, 2)
    pick(1, 2, -2)
    send_rows(1, 1)
    build(4)
    build_kron()
    ring_forward(0, 3)
    ring_begin(2)
    pick(0, 3, -3)
    ring_forward(1, 3)
    ring_begin(3)
    pick(1, 3, -3)
    hid_pass()
    ring_forward(0, 4)
    pick(0, 4)
    send_rows(0, 2)
    ring_forward(2, 1)
    own_wait(2)
    pick(2, 0, 1, -1)
    ring_forward(1, 4)
    pick(1, 4)
    ring_forward(3, 1)
    hid_near()
    matmul_near()
    ring_forward(2, 2)
    hid_far()
    matmul_far()
    send_rows(1, 2)
    pick(2, 2, -2)
    ring_forward(3, 2)
    own_wait(3)
    pick(3, 0, 1, -1)
    ring_forward(2, 3)
    stage_forward(0)
    ring_forward(3, 3)
    stage_matmul(1)
    send_rows(2, 0)
    pick(3, 2, -2)
    pick(2, 3, -3)
    send_rows(2, 1)
    send_rows(3, 0)
    pick(3, 3, -3)
    send_rows(3, 1)
    ring_forward(2, 4)
    pick(2, 4)
    send_rows(2, 2)
    stage_forward(1)
    ring_forward(3, 4)
    pick(3, 4)
    send_rows(3, 2)
    latent_begin()
    stage_adam(0)
    stage_matmul(2)
    stage_matmul(3)
    stage_adam(1)
    stage_forward(2)
    stage_forward(3)
    stage_return(0)
    latent_end()
    stage_adam(2)
    drain_start()
    stage_return(1)
    stage_adam(3)
    drain_parts()
    stage_return(2)
    drain_out(0)
    drain_out(1)
    step_sent(2)
    stage_return(3)
    step_sent(3)
    drain_out(2)
    drain_out(3)


def expert_steps(*operands):
    anywhere = pl.BlockSpec(memory_space=pl.ANY)
    relays = [
        jax.ShapeDtypeStruct((2, PEERS, PLANES, ROWS, dc), BF16) for _, dc in CHUNKS
    ]
    returns = [
        jax.ShapeDtypeStruct((2, PLANES, PEERS, ROWS, dc), BF16) for _, dc in CHUNKS[: N - 1]
    ]
    shape = jax.ShapeDtypeStruct((2, PLANES, PEERS, ROWS, WIDTH), BF16)
    widest = max(dc for _, dc in CHUNKS)
    dma = pltpu.SemaphoreType.DMA
    scratch = [pltpu.VMEM((PLANES, TOKENS, dc), BF16) for _, dc in CHUNKS]
    scratch += [pltpu.VMEM((2, PEERS, PLANES, POS, dc), BF16) for _, dc in CHUNKS]
    scratch += [pltpu.VMEM((2, PLANES, PEERS, ROWS, dc), BF16) for _, dc in CHUNKS]
    scratch += [pltpu.VMEM((PEERS, 2, PLANES, POS, dc), BF16) for _, dc in CHUNKS]
    scratch += [pltpu.VMEM((2, PLANES, PEERS, ROWS, dc), BF16) for _, dc in CHUNKS[N - 1 :]]
    scratch += [
        pltpu.VMEM((PLANES, 4, TOKENS), jnp.int32),
        pltpu.VMEM((PLANES, 4, TOKENS), F32),
        pltpu.VMEM((PLANES, 16 * POS, TOKENS), BF16),
        pltpu.VMEM((2, 16 * POS, NEED), BF16),
        pltpu.VMEM((PLANES, 16 * POS, 128), F32),
        pltpu.VMEM((2, 4, PEERS, FPART, PLANES * POS), BF16),
        pltpu.VMEM((2, PEERS, 2, PLANES, ROWS, widest), BF16),
        pltpu.VMEM((2, 2, PLANES, PEERS, ROWS, widest), BF16),
        pltpu.VMEM((2, 2, PLANES * PEERS * ROWS, widest), BF16),
        pltpu.VMEM((1024, 1024), BF16),
        pltpu.VMEM((1024, 1024), BF16),
        pltpu.VMEM((TOKENS, TOKENS), BF16),
        pltpu.VMEM((PLANES * PEERS, CAP, 2, FPART), BF16),
        pltpu.VMEM((TOKENS, 1024), BF16),
        pltpu.VMEM((512, 1024), BF16),
        pltpu.VMEM((4, 128, TOKENS), F32),
        pltpu.VMEM((3, 128, TOKENS), F32),
        dma((2, 2)),
        dma((N, 2, 4, 2)),
        dma((2, N)),
        dma((7,)),
        dma((2, N)),
        dma((2, N)),
        dma((2, N)),
        dma((2, N)),
        dma((2, 8)),
        dma((2, N)),
        dma((2,)),
        dma((N + 9,)),
        dma((5, N)),
    ]
    results = pl.pallas_call(
        kernel,
        out_shape=[shape, jax.ShapeDtypeStruct((128, TOKENS), BF16)] + relays + returns,
        in_specs=[anywhere] * 4 + [pl.BlockSpec(memory_space=pltpu.VMEM)] + [anywhere] * 4,
        out_specs=[anywhere] * (2 * N + 1),
        scratch_shapes=scratch,
        compiler_params=pltpu.CompilerParams(
            collective_id=0, has_side_effects=True, vmem_limit_bytes=62 * 1024 * 1024
        ),
        cost_estimate=pl.CostEstimate(
            flops=50_000_000_000, bytes_accessed=60_000_000, transcendentals=2_000_000
        ),
    )(*operands)
    return results[0], results[1]


def hand_over_kernel(steps, latent, steps_out, latent_out, steps_held, latent_held, sem):
    pieces = [
        (steps.at[w, i], steps_held.at[w, i], steps_out.at[w, i])
        for w in range(2)
        for i in range(PLANES)
    ]
    pieces.append((latent, latent_held, latent_out))
    into = [
        pltpu.make_async_copy(a, b, sem.at[0, n]) for n, (a, b, _) in enumerate(pieces)
    ]
    back = [
        pltpu.make_async_copy(b, c, sem.at[1, n]) for n, (_, b, c) in enumerate(pieces)
    ]
    for copy in into:
        copy.start()
    for first, second in zip(into, back):
        first.wait()
        second.start()
    for copy in back:
        copy.wait()


def hand_over(*results):
    anywhere = pl.BlockSpec(memory_space=pl.ANY)
    return pl.pallas_call(
        hand_over_kernel,
        out_shape=[jax.ShapeDtypeStruct(r.shape, r.dtype) for r in results],
        in_specs=[anywhere] * 2,
        out_specs=[anywhere] * 2,
        scratch_shapes=[pltpu.VMEM(r.shape, r.dtype) for r in results]
        + [pltpu.SemaphoreType.DMA((2, 2 * PLANES + 1))],
    )(*results)


def shards(out_grad, routes, gates, dup_owner, hidden, moment1, moment2, value_grad, value_proj):
    experts = PLANES * PEERS
    hid = hidden[0].transpose(0, 2, 1, 3)
    steps, latent_grad = expert_steps(
        out_grad,
        routes.T,
        gates.T,
        hid,
        dup_owner.reshape(1, -1),
        moment1.reshape(experts * ROWS, WIDTH),
        moment2.reshape(experts * ROWS, WIDTH),
        value_grad,
        value_proj,
    )
    steps, latent_grad = hand_over(steps, latent_grad)
    return (steps.reshape(1, 2, PLANES * PEERS * ROWS, WIDTH), latent_grad)


def solution(mesh):
    in_specs = (
        P("expert", "dp"),
        P("expert", None),
        P("expert", None),
        P(),
        P("expert", None, None, None, "dp"),
        P(None, "expert", "dp"),
        P(None, "expert", "dp"),
        P("expert", "dp"),
        P(None, "dp"),
    )
    out_specs = (P("expert", None, None, "dp"), P("dp", "expert"))
    return jax.shard_map(shards, mesh=mesh, in_specs=in_specs, out_specs=out_specs, check_vma=False)
```
